512 devices in a mesh: layer: 8 (over y, core), feat: 16 (over z_hi, x), width: 4 (over z_lo).
Axes of the slice: x: 4, y: 4, z: 16 (z_hi: 4, z_lo: 4; z = z_hi * 4 + z_lo), core: 2. Of those that a mesh axis runs over, the one named last changes fastest.
Arguments:
- resid: bfloat16 [2, 128, 2048], P(None, 'layer', 'width'), may hold values from -6 to 6
- enc_w: bfloat16 [2, 2048, 65536], P(None, 'width', ('layer', 'feat')), may hold values from -0.125 to 0.125
- enc_b: float32 [2, 65536], P(None, ('layer', 'feat')), may hold values from -3 to 3
- dec_w: float32 [3, 65536, 2048], P(None, ('layer', 'feat'), 'width'), may hold values from -0.09375 to 0.09375
- dec_b: float32 [2, 2048], P(None, 'width'), may hold values from -2 to 2
- target: float32 [2, 128, 2048], P(None, ('layer', 'feat'), 'width'), may hold values from -6 to 6
Outputs:
- recon: float32 [2, 128, 2048], P(None, ('layer', 'feat'), 'width')
- err: float32 [2, 128], P(None, ('layer', 'feat'))
The draws below stay inside these ranges and needn't reach their ends.
All inputs are finite; a program needn't handle non-finite values.
Results may differ from the reference program's by a relative error of at most 0.00035.
Values may be sent and summed in bfloat16 or wider, within the bound.
A program may use at most 64 MiB of HBM per device.

```python
import jax
import jax.numpy as jnp
from jax import lax

D = 2048
FEATURES = 65536
LAYERS = 2
TOKENS = 128
BLOCKS = 3


def raised(array, own_key, source, target, shards_of, factor):
    owner, partner = [(jnp.arange(array.shape[position]) // (array.shape[position] // shards_of)).reshape([-1 if axis == position else 1 for axis in range(array.ndim)]) for position in (source, target)]
    chosen = jax.random.permutation(own_key, shards_of)[partner]
    strong = (owner == chosen) | (owner == (partner + shards_of // 2) % shards_of)
    return jnp.where(strong, factor * array, array)


def block_scale(rng, shape, split, low, top_value):
    level = 1.0
    for position, shards_of in split:
        heights = jax.random.uniform(jax.random.fold_in(jax.random.fold_in(rng, 6), position), (shards_of,), jnp.float32, low / len(split), top_value / len(split))
        level = level * jnp.repeat(jnp.exp(heights), shape[position] // shards_of).reshape((-1,) + (1,) * (len(shape) - 1 - position))
    return level


def scatter_about(stream_key, dims, width, bound, split=(), kind=jnp.bfloat16):
    level = block_scale(stream_key, dims, split, -0.22, 0.18) if split else 1.0
    result = jax.random.normal(stream_key, dims, jnp.float32) * width * level
    return jnp.minimum(jnp.maximum(result, -bound), bound).astype(kind)


def heavy_noise(key, extent, spread, reach, cuts, heavy, dtype=jnp.bfloat16):
    result = spread * jax.random.normal(key, extent, jnp.float32)
    if cuts:
        result = result * block_scale(key, extent, cuts, -0.22, 0.18)
    return jnp.clip(raised(result, jax.random.fold_in(key, 3), *heavy), -reach, reach).astype(dtype)


def setup_inputs(seed: int = 0) -> dict:
    arg_keys = jax.random.split(jax.random.key(seed), 7)
    return {
        "resid": scatter_about(arg_keys[0], (LAYERS, TOKENS, D), 1.0, 6.0, ((1, 8), (2, 4))),
        "enc_w": scatter_about(arg_keys[1], (LAYERS, D, FEATURES), D ** -0.5, 0.125, ((1, 4), (2, 128))),
        "enc_b": scatter_about(arg_keys[2], (LAYERS, FEATURES), 0.5, 3.0, ((1, 128),), jnp.float32),
        "dec_w": heavy_noise(arg_keys[3], (BLOCKS, FEATURES, D), FEATURES ** -0.5, 0.09375, ((1, 128), (2, 4)), (1, 2, 128, 5.5), jnp.float32),
        "dec_b": scatter_about(arg_keys[4], (LAYERS, D), 0.3, 2.0, ((1, 4),), jnp.float32),
        "target": scatter_about(arg_keys[5], (LAYERS, TOKENS, D), 1.0, 6.0, ((1, 128), (2, 4)), jnp.float32),
    }


def reference(resid, enc_w, enc_b, dec_w, dec_b, target):
    acts = []
    for layer_idx in range(LAYERS):
        pre = jnp.dot(resid[layer_idx], enc_w[layer_idx], preferred_element_type=jnp.float32) + enc_b[layer_idx][None, :]
        acts.append(jnp.maximum(pre, 0.0))
    outs = []
    for target_idx in range(LAYERS):
        total = jnp.zeros((TOKENS, D), jnp.float32) + dec_b[target_idx][None, :]
        for layer_idx in range(target_idx + 1):
            block = target_idx * (target_idx + 1) // 2 + layer_idx
            total = total + jnp.dot(acts[layer_idx], dec_w[block], precision=lax.Precision.HIGHEST, preferred_element_type=jnp.float32)
        outs.append(total)
    recon = jnp.stack(outs, 0)
    diff = recon - target
    err = jnp.sum(diff * diff, axis=2) / (jnp.sum(target * target, axis=2) + 1e-6)
    return recon, err
```

```python
import functools

import jax
import jax.numpy as jnp
from jax import lax
from jax.experimental import pallas as pl
from jax.experimental.pallas import tpu as pltpu
from jax.sharding import PartitionSpec as P

MESH = pl.DeviceIdType.MESH
F32 = jnp.float32
BF16 = jnp.bfloat16
CORES = 2
SIDE = 4
CHUNKS = 4


def block_of(target_idx, layer_idx):
    return target_idx * (target_idx + 1) // 2 + layer_idx


def kernel(
    layers,
    resid,
    enc_w,
    enc_b,
    dec_w,
    dec_b,
    target,
    recon,
    err,
    own_in,
    rows,
    ew,
    eb,
    dw,
    dw_hi,
    dw_lo,
    db,
    tg,
    part,
    heard,
    act,
    total,
    core_in,
    pair,
    plane_in,
    plane,
    deep_in,
    squares,
    in_sem,
    ew_sem,
    dw_sem,
    gather_sem,
    part_sem,
    act_sem,
    core_sem,
    plane_sem,
    own_sem,
    deep_sem,
    square_sem,
):
    me_layer = lax.axis_index("layer")
    me_feat = lax.axis_index("feat")
    me_width = lax.axis_index("width")
    y, core = me_layer // CORES, me_layer % CORES
    deep, x = me_feat // SIDE, me_feat % SIDE
    group = SIDE * CORES
    own_rows = own_in.shape[1]
    features = ew.shape[2]
    fc = features // CHUNKS
    width = dw.shape[2]
    steps = layers * CHUNKS

    is_mid = jnp.logical_and(me_width >= 1, me_width <= 2)
    is_end = jnp.logical_not(is_mid)
    kind = jnp.where(is_mid, 1, 0)
    forward = jnp.where(jnp.logical_or(me_width == 0, me_width == 2), 1, 2)
    outer = jnp.where(me_width == 1, 0, 3)

    local = [
        pltpu.make_async_copy(resid, own_in, in_sem.at[0]),
        pltpu.make_async_copy(enc_b, eb, in_sem.at[1]),
        pltpu.make_async_copy(dec_b, db, in_sem.at[2]),
        pltpu.make_async_copy(target, tg, in_sem.at[3]),
    ]
    enc_loads = [pltpu.make_async_copy(enc_w.at[l], ew.at[l], ew_sem.at[l]) for l in range(layers)]
    blocks = dw.shape[0]
    dec_loads = [pltpu.make_async_copy(dec_w.at[b], dw.at[b], dw_sem.at[b]) for b in range(blocks)]
    local[0].start()
    enc_loads[0].start()
    for copy in local[1:]:
        copy.start()
    for copy in dec_loads[: blocks - 1]:
        copy.start()
    for copy in enc_loads[1:]:
        copy.start()
    dec_loads[blocks - 1].start()

    barrier = pltpu.get_barrier_semaphore()

    def greet(layer, feat, wid):
        pl.semaphore_signal(barrier, inc=1, device_id=(layer, feat, wid), device_id_type=MESH)

    def greet_layer(d, carry):
        greet((me_layer + d) % group, me_feat, me_width)
        return carry

    def greet_plane(d, carry):
        to_y = (y + d // (SIDE - 1)) % SIDE
        to_x = (x + 1 + d % (SIDE - 1)) % SIDE
        greet(to_y * CORES + core, deep * SIDE + to_x, me_width)
        return carry

    def greet_deep(d, carry):
        greet(me_layer, ((deep + d) % SIDE) * SIDE + x, me_width)
        return carry

    def greet_width(d, carry):
        greet(me_layer, me_feat, (me_width + d) % SIDE)
        return carry

    lax.fori_loop(1, group, greet_layer, 0)
    lax.fori_loop(0, SIDE * (SIDE - 1), greet_plane, 0)
    lax.fori_loop(1, SIDE, greet_deep, 0)
    lax.fori_loop(1, SIDE, greet_width, 0)

    local[0].wait()
    place = lax.broadcasted_iota(jnp.int32, (own_rows, own_rows), 0)
    source = lax.broadcasted_iota(jnp.int32, (own_rows, own_rows), 1)
    swap = jnp.where(source == (place % SIDE) * SIDE + place // SIDE, 1.0, 0.0).astype(BF16)
    own = pl.ds(pl.multiple_of(me_layer * own_rows, own_rows), own_rows)
    for l in range(layers):
        swapped = jnp.dot(swap, own_in[l], preferred_element_type=F32)
        rows[l, own, :] = swapped.astype(BF16)

    pl.semaphore_wait(barrier, group - 1 + SIDE * (SIDE - 1) + 2 * (SIDE - 1))

    for l in range(layers):

        def push(d, carry, l=l):
            pltpu.make_async_remote_copy(
                src_ref=rows.at[l, own, :],
                dst_ref=rows.at[l, own, :],
                send_sem=gather_sem.at[0, l],
                recv_sem=gather_sem.at[1, l],
                device_id=((me_layer + d) % group, me_feat, me_width),
                device_id_type=MESH,
            ).start()
            return carry

        lax.fori_loop(1, group, push, 0)

    def gather_wait(way, l):
        some = rows.at[l, pl.ds(0, (group - 1) * own_rows), :]
        pltpu.make_async_copy(some, some, gather_sem.at[way, l]).wait()

    def split(b):
        dec_loads[b].wait()
        step = 64

        def body(i, carry):
            at = pl.ds(pl.multiple_of(i * step, step), step)
            whole = dw[b, at, :]
            high = whole.astype(BF16)
            dw_hi[b, at, :] = high
            dw_lo[b, at, :] = (whole - high.astype(F32)).astype(BF16)
            return carry

        lax.fori_loop(0, features // step, body, 0)

    for b in range(blocks - 1):
        split(b)

    def send_part(q):
        return pltpu.make_async_remote_copy(
            src_ref=part.at[q],
            dst_ref=heard.at[kind, q],
            send_sem=part_sem.at[0, kind, q],
            recv_sem=part_sem.at[1, kind, q],
            device_id=(me_layer, me_feat, forward),
            device_id_type=MESH,
        )

    def wait_part(k, q):
        pltpu.make_async_copy(heard.at[k, q], heard.at[k, q], part_sem.at[1, k, q]).wait()

    def send_act(q):
        return pltpu.make_async_remote_copy(
            src_ref=act.at[q],
            dst_ref=act.at[q],
            send_sem=act_sem.at[0, q],
            recv_sem=act_sem.at[1, q],
            device_id=(me_layer, me_feat, outer),
            device_id_type=MESH,
        )

    def encode(l):
        for h in range(CHUNKS):
            q = l * CHUNKS + h
            part[q] = jnp.dot(
                rows[l], ew[l, :, h * fc : (h + 1) * fc], preferred_element_type=F32
            )

            @pl.when(is_end)
            def _():
                send_part(q).start()

    def pass_on(q):
        @pl.when(is_mid)
        def _():
            wait_part(0, q)
            part[q] = part[q] + heard[0, q]
            send_part(q).start()

    def finish(q):
        l, h = divmod(q, CHUNKS)

        @pl.when(is_mid)
        def _():
            wait_part(1, q)
            bias = eb[l : l + 1, h * fc : (h + 1) * fc]
            act[q] = jnp.maximum(part[q] + heard[1, q] + bias, 0.0)
            send_act(q).start()

        @pl.when(is_end)
        def _():
            pltpu.make_async_copy(act.at[q], act.at[q], act_sem.at[1, q]).wait()

    def decode(q):
        l, h = divmod(q, CHUNKS)
        whole = act[q]
        high = whole.astype(BF16)
        low = (whole - high.astype(F32)).astype(BF16)
        for m in range(l, layers):
            b = block_of(m, l)
            w_hi = dw_hi[b, h * fc : (h + 1) * fc, :]
            w_lo = dw_lo[b, h * fc : (h + 1) * fc, :]
            term = jnp.dot(high, w_hi, preferred_element_type=F32)
            term += jnp.dot(low, w_hi, preferred_element_type=F32)
            term += jnp.dot(high, w_lo, preferred_element_type=F32)
            term = term.reshape(total.shape[1:])
            if q == 0:
                total[m] = term
            else:
                total[m] += term

    def send_core(m):
        return pltpu.make_async_remote_copy(
            src_ref=total.at[m, :, 1 - core],
            dst_ref=core_in.at[m],
            send_sem=core_sem.at[0, m],
            recv_sem=core_sem.at[1, m],
            device_id=(y * CORES + 1 - core, me_feat, me_width),
            device_id_type=MESH,
        )

    def own_plane(m):
        return pltpu.make_async_copy(pair.at[m, y * SIDE + x], plane_in.at[m, 0], own_sem.at[m])

    def send_plane(m, d):
        to_y, to_x = (y + d // SIDE) % SIDE, (x + d % SIDE) % SIDE
        return pltpu.make_async_remote_copy(
            src_ref=pair.at[m, to_y * SIDE + to_x],
            dst_ref=plane_in.at[m, d],
            send_sem=plane_sem.at[0, m],
            recv_sem=plane_sem.at[1, m],
            device_id=(to_y * CORES + core, deep * SIDE + to_x, me_width),
            device_id_type=MESH,
        )

    def plane_wait(way, m):
        some = plane_in.at[m, pl.ds(1, SIDE * SIDE - 1)]
        pltpu.make_async_copy(some, some, plane_sem.at[way, m]).wait()

    def send_deep(m, d):
        to = (deep + d) % SIDE
        return pltpu.make_async_remote_copy(
            src_ref=plane.at[m, to],
            dst_ref=deep_in.at[m, d],
            send_sem=deep_sem.at[0, m],
            recv_sem=deep_sem.at[1, m],
            device_id=(me_layer, to * SIDE + x, me_width),
            device_id_type=MESH,
        )

    def deep_wait(way, m):
        some = deep_in.at[m, pl.ds(1, SIDE - 1)]
        pltpu.make_async_copy(some, some, deep_sem.at[way, m]).wait()

    def start_plane(m):
        send_core(m).wait_recv()
        for to_y in range(SIDE):
            both = total[m, to_y, core] + core_in[m, to_y]
            for to_x in range(SIDE):
                pair[m, to_y * SIDE + to_x] = both[to_x * SIDE : (to_x + 1) * SIDE]
        own_plane(m).start()

        def body(d, carry):
            send_plane(m, d).start()
            return carry

        lax.fori_loop(1, SIDE * SIDE, body, 0)

    def start_deep(m):
        own_plane(m).wait()
        plane_wait(1, m)
        summed = jnp.sum(plane_in[m], axis=0)
        for to in range(SIDE):
            plane[m, to] = summed[to : to + 1]

        def body(d, carry):
            send_deep(m, d).start()
            return carry

        lax.fori_loop(1, SIDE, body, 0)

    def result(m):
        deep_wait(1, m)
        summed = plane[m, deep]
        for d in range(1, SIDE):
            summed = summed + deep_in[m, d]
        summed = summed + db[m : m + 1]
        recon[m] = summed
        diff = summed - tg[m]
        sq_error = jnp.sum(diff * diff, axis=1, keepdims=True)
        sq_target = jnp.sum(tg[m] * tg[m], axis=1, keepdims=True)
        lanes = squares.shape[2]
        squares[me_width, m : m + 1, :] = jnp.broadcast_to(sq_error, (1, lanes))
        squares[me_width, layers + m : layers + m + 1, :] = jnp.broadcast_to(sq_target, (1, lanes))

    gather_wait(1, 0)
    enc_loads[0].wait()
    encode(0)
    ahead = 2
    for q in range(ahead):
        pass_on(q)
    gather_wait(1, 1)
    enc_loads[1].wait()
    encode(1)
    split(blocks - 1)
    for copy in local[1:]:
        copy.wait()
    squares[me_width] = jnp.zeros(squares.shape[1:], F32)
    for q in range(steps):
        finish(q)
        if q + ahead < steps:
            pass_on(q + ahead)
        decode(q)
        if q == CHUNKS - 1:
            send_core(0).start()
        if q == CHUNKS:
            start_plane(0)
        if q == steps - 2:
            start_deep(0)
    send_core(1).start()
    result(0)
    start_plane(1)
    start_deep(1)
    result(1)

    def send_squares(d):
        return pltpu.make_async_remote_copy(
            src_ref=squares.at[me_width],
            dst_ref=squares.at[me_width],
            send_sem=square_sem.at[0, d],
            recv_sem=square_sem.at[1, d],
            device_id=(me_layer, me_feat, (me_width + d) % SIDE),
            device_id_type=MESH,
        )

    for d in range(1, SIDE):
        send_squares(d).start()
    for d in range(1, SIDE):
        send_squares(d).wait_recv()
    sums = jnp.sum(squares[...], axis=0)
    err[...] = sums[0:layers, 0:1] / (sums[layers : 2 * layers, 0:1] + 1e-06)

    for d in range(1, SIDE):
        send_squares(d).wait_send()
    for m in range(layers):
        gather_wait(0, m)
        send_core(m).wait_send()
        plane_wait(0, m)
        deep_wait(0, m)
    for q in range(steps):
        send_part(q).wait_send()

        @pl.when(is_mid)
        def _():
            send_act(q).wait_send()


def per_device(resid, enc_w, enc_b, dec_w, dec_b, target):
    layers, own_rows, wide = resid.shape
    features = enc_w.shape[2]
    blocks, _, width = dec_w.shape
    group = SIDE * CORES
    tokens = group * own_rows
    fc = features // CHUNKS
    steps = layers * CHUNKS
    vm = pltpu.VMEM
    dma = pltpu.SemaphoreType.DMA
    anywhere = pl.BlockSpec(memory_space=pl.ANY)
    in_vmem = pl.BlockSpec(memory_space=pltpu.VMEM)
    return pl.pallas_call(
        functools.partial(kernel, layers),
        out_shape=(
            jax.ShapeDtypeStruct((layers, 1, width), F32),
            jax.ShapeDtypeStruct((layers, 1), F32),
        ),
        in_specs=[anywhere] * 6,
        out_specs=(in_vmem, in_vmem),
        scratch_shapes=[
            vm((layers, own_rows, wide), BF16),
            vm((layers, tokens, wide), BF16),
            vm((layers, wide, features), BF16),
            vm((layers, features), F32),
            vm((blocks, features, width), F32),
            vm((blocks, features, width), BF16),
            vm((blocks, features, width), BF16),
            vm((layers, width), F32),
            vm((layers, 1, width), F32),
            vm((steps, tokens, fc), F32),
            vm((2, steps, tokens, fc), F32),
            vm((steps, tokens, fc), F32),
            vm((layers, SIDE, CORES, own_rows, width), F32),
            vm((layers, SIDE, own_rows, width), F32),
            vm((layers, SIDE * SIDE, SIDE, width), F32),
            vm((layers, SIDE * SIDE, SIDE, width), F32),
            vm((layers, SIDE, 1, width), F32),
            vm((layers, SIDE, 1, width), F32),
            vm((SIDE, 8, 128), F32),
            dma((4,)),
            dma((layers,)),
            dma((blocks,)),
            dma((2, layers)),
            dma((2, 2, steps)),
            dma((2, steps)),
            dma((2, layers)),
            dma((2, layers)),
            dma((layers,)),
            dma((2, layers)),
            dma((2, SIDE)),
        ],
        compiler_params=pltpu.CompilerParams(
            collective_id=0, has_side_effects=True, vmem_limit_bytes=48 * 1024 * 1024
        ),
        cost_estimate=pl.CostEstimate(
            flops=1_400_000_000, bytes_accessed=4_500_000, transcendentals=0
        ),
    )(resid, enc_w, enc_b, dec_w, dec_b, target)


def solution(mesh):
    in_specs = (
        P(None, "layer", "width"),
        P(None, "width", ("layer", "feat")),
        P(None, ("layer", "feat")),
        P(None, ("layer", "feat"), "width"),
        P(None, "width"),
        P(None, ("layer", "feat"), "width"),
    )
    out_specs = (P(None, ("layer", "feat"), "width"), P(None, ("layer", "feat")))
    return jax.shard_map(
        per_device, mesh=mesh, in_specs=in_specs, out_specs=out_specs, check_vma=False
    )
```

```python
import functools

import jax
import jax.numpy as jnp
from jax import lax
from jax.experimental import pallas as pl
from jax.experimental.pallas import tpu as pltpu
from jax.sharding import PartitionSpec as P

MESH = pl.DeviceIdType.MESH
F32 = jnp.float32
BF16 = jnp.bfloat16
CORES = 2
SIDE = 4
SHIFTS = (0, 1, 3, 2)

WIRE = BF16
POWER = 12.0
BASE = 124.0
FINE = 2.0**-10


def to_wire(value):
    size = jnp.exp2(jnp.log2(jnp.abs(value) * (1.0 / FINE) + 1.0) * POWER - BASE)
    return jnp.where(value < 0.0, -size, size).astype(WIRE)


def from_wire(code):
    code = code.astype(F32)
    size = jnp.exp2((jnp.log2(jnp.abs(code)) + BASE) * (1.0 / POWER)) * FINE - FINE
    return jnp.where(code < 0.0, -size, size)


def block_of(target_idx, layer_idx):
    return target_idx * (target_idx + 1) // 2 + layer_idx


def kernel(
    layers,
    resid,
    enc_w,
    enc_b,
    dec_w,
    dec_b,
    target,
    recon,
    err,
    own_in,
    rows,
    ew,
    eb,
    dw,
    dw_hi,
    dw_lo,
    db,
    tg,
    part,
    outgoing,
    heard,
    act_wire,
    act,
    total,
    core_in,
    pair,
    plane_in,
    plane,
    deep_in,
    side,
    in_sem,
    ew_sem,
    dw_sem,
    gather_sem,
    part_sem,
    act_sem,
    core_sem,
    plane_sem,
    own_sem,
    deep_sem,
    side_sem,
    know_sem,
):
    me_layer = lax.axis_index("layer")
    me_feat = lax.axis_index("feat")
    me_width = lax.axis_index("width")
    y, core = me_layer // CORES, me_layer % CORES
    deep, x = me_feat // SIDE, me_feat % SIDE
    group = SIDE * CORES
    own_rows = own_in.shape[1]
    features = ew.shape[2]
    blocks = dw.shape[0]
    chunk_rows = CORES * own_rows

    is_low = me_width == 0
    is_high = me_width == SIDE - 1
    is_end = jnp.logical_or(is_low, is_high)
    is_mid = jnp.logical_not(is_end)
    kind = jnp.where(is_mid, 1, 0)
    forward = jnp.where(jnp.logical_or(me_width == 0, me_width == 2), 1, 2)
    outer = jnp.where(me_width == 1, 0, 3)
    beside = jnp.where(is_low, (deep + SIDE - 1) % SIDE, (deep + 1) % SIDE) * SIDE + x

    def signal(sem, layer, feat, wid):
        pl.semaphore_signal(sem, inc=1, device_id=(layer, feat, wid), device_id_type=MESH)

    barrier = pltpu.get_barrier_semaphore()

    def greet_layer(d, carry):
        signal(barrier, (me_layer + d) % group, me_feat, me_width)
        return carry

    def greet_others(d, carry):
        signal(barrier, me_layer, me_feat, (me_width + d) % SIDE)
        signal(barrier, me_layer, deep * SIDE + (x + d) % SIDE, me_width)
        return carry

    load_rows = pltpu.make_async_copy(resid, own_in, in_sem.at[0])
    load_rows.start()
    lax.fori_loop(1, group, greet_layer, 0)
    lax.fori_loop(1, SIDE, greet_others, 0)

    @pl.when(is_end)
    def _():
        signal(barrier, me_layer, beside, SIDE - 1 - me_width)

    load_bias = pltpu.make_async_copy(enc_b, eb, in_sem.at[1])
    load_db = pltpu.make_async_copy(dec_b, db, in_sem.at[2])
    load_tg = pltpu.make_async_copy(target, tg, in_sem.at[3])
    load_enc = [pltpu.make_async_copy(enc_w.at[l], ew.at[l], ew_sem.at[l]) for l in range(layers)]
    load_dec = [pltpu.make_async_copy(dec_w.at[b], dw.at[b], dw_sem.at[b]) for b in range(blocks)]
    for copy in load_enc + load_dec + [load_bias, load_db, load_tg]:
        copy.start()

    load_rows.wait()
    place = lax.broadcasted_iota(jnp.int32, (own_rows, own_rows), 0)
    source = lax.broadcasted_iota(jnp.int32, (own_rows, own_rows), 1)
    swap = jnp.where(source == (place % SIDE) * SIDE + place // SIDE, 1.0, 0.0).astype(BF16)
    for l in range(layers):
        swapped = jnp.dot(swap, own_in[l], preferred_element_type=F32)
        rows[me_layer, l] = swapped.astype(BF16)

    near = group - 1 + 2 * (SIDE - 1)
    pl.semaphore_wait(barrier, jnp.where(is_end, near + 1, near))

    def push(k, to_core):
        to = ((y + SHIFTS[k]) % SIDE) * CORES + to_core
        pltpu.make_async_remote_copy(
            src_ref=rows.at[me_layer],
            dst_ref=rows.at[me_layer],
            send_sem=gather_sem.at[0, 0],
            recv_sem=gather_sem.at[1, SHIFTS.index((SIDE - SHIFTS[k]) % SIDE)],
            device_id=(to, me_feat, me_width),
            device_id_type=MESH,
        ).start()

    push(0, 1 - core)
    for k in (3, 1, 2):
        push(k, core)
        push(k, 1 - core)

    def gather_wait(way, k, count):
        some = rows.at[pl.ds(0, count)]
        pltpu.make_async_copy(some, some, gather_sem.at[way, k]).wait()

    def greet_row(d, carry):
        signal(know_sem.at[4], me_layer, deep * SIDE + (x + d) % SIDE, me_width)
        return carry

    lax.fori_loop(1, SIDE, greet_row, 0)

    @pl.when(is_end)
    def _():
        signal(know_sem.at[0], me_layer, beside, SIDE - 1 - me_width)

    def know_lines(step):
        @pl.when(is_end)
        def _():
            pl.semaphore_wait(know_sem.at[step], 1)
            if step == 0:
                signal(know_sem.at[1], me_layer, me_feat, SIDE - 1 - me_width)
            elif step == 1:
                signal(know_sem.at[2], me_layer, beside, SIDE - 1 - me_width)
            else:
                signal(know_sem.at[3], me_layer, me_feat, forward)

    def split(b):
        load_dec[b].wait()
        step = 64

        def body(i, carry):
            at = pl.ds(pl.multiple_of(i * step, step), step)
            whole = dw[b, at, :]
            high = whole.astype(BF16)
            dw_hi[b, at, :] = high
            dw_lo[b, at, :] = (whole - high.astype(F32)).astype(BF16)
            return carry

        lax.fori_loop(0, features // step, body, 0)

    def send_part(k, l):
        return pltpu.make_async_remote_copy(
            src_ref=outgoing.at[k, l],
            dst_ref=heard.at[kind, k, l],
            send_sem=part_sem.at[0, k, l],
            recv_sem=part_sem.at[1 + kind, k, l],
            device_id=(me_layer, me_feat, forward),
            device_id_type=MESH,
        )

    def wait_part(which, k, l):
        some = heard.at[which, k, l]
        pltpu.make_async_copy(some, some, part_sem.at[1 + which, k, l]).wait()

    def send_act(k, l):
        return pltpu.make_async_remote_copy(
            src_ref=act_wire.at[k, l],
            dst_ref=act_wire.at[k, l],
            send_sem=act_sem.at[0, k, l],
            recv_sem=act_sem.at[1, k, l],
            device_id=(me_layer, me_feat, outer),
            device_id_type=MESH,
        )

    def encode(k):
        gather_wait(1, k, CORES if k else 1)
        first = ((y + SHIFTS[k]) % SIDE) * CORES
        for l in range(layers):
            if k == 0:
                load_enc[l].wait()
            some = rows[pl.ds(first, CORES), l].reshape(chunk_rows, -1)
            partial = jnp.dot(some, ew[l], preferred_element_type=F32)

            @pl.when(is_end)
            def _(l=l, partial=partial):
                outgoing[k, l] = to_wire(partial)
                send_part(k, l).start()

            @pl.when(is_mid)
            def _(l=l, partial=partial):
                part[k, l] = partial

    def pass_on(k):
        @pl.when(is_mid)
        def _():
            for l in range(layers):
                wait_part(0, k, l)
                summed = part[k, l] + from_wire(heard[0, k, l])
                outgoing[k, l] = to_wire(summed)
                send_part(k, l).start()
                part[k, l] = summed

    def finish(k):
        for l in range(layers):

            @pl.when(is_mid)
            def _(l=l):
                wait_part(1, k, l)
                pre = part[k, l] + from_wire(heard[1, k, l]) + eb[l : l + 1, :]
                pre = jnp.maximum(pre, 0.0)
                act_wire[k, l] = to_wire(pre)
                send_act(k, l).start()
                act[l] = pre

            @pl.when(is_end)
            def _(l=l):
                some = act_wire.at[k, l]
                pltpu.make_async_copy(some, some, act_sem.at[1, k, l]).wait()
                act[l] = from_wire(act_wire[k, l])

            decode(k, l)

    def decode(k, l):
        whole = act[l]
        high = whole.astype(BF16)
        low = (whole - high.astype(F32)).astype(BF16)
        both = jnp.concatenate([high, low], axis=0)
        for m in range(l, layers):
            b = block_of(m, l)
            twice = jnp.dot(both, dw_hi[b], preferred_element_type=F32)
            term = twice[:chunk_rows] + twice[chunk_rows:]
            term += jnp.dot(high, dw_lo[b], preferred_element_type=F32)
            term = term.reshape(CORES, own_rows, -1)
            if l == 0:
                total[k, m] = term
            else:
                total[k, m] += term

    def send_core(k):
        return pltpu.make_async_remote_copy(
            src_ref=total.at[k, :, 1 - core],
            dst_ref=core_in.at[k],
            send_sem=core_sem.at[0, k],
            recv_sem=core_sem.at[1, k],
            device_id=(y * CORES + 1 - core, me_feat, me_width),
            device_id_type=MESH,
        )

    own_plane = pltpu.make_async_copy(pair.at[0, x], plane_in.at[y * SIDE + x], own_sem.at[0])

    def send_plane(k, to_x):
        return pltpu.make_async_remote_copy(
            src_ref=pair.at[k, to_x],
            dst_ref=plane_in.at[y * SIDE + x],
            send_sem=plane_sem.at[0],
            recv_sem=plane_sem.at[1],
            device_id=(((y + SHIFTS[k]) % SIDE) * CORES + core, deep * SIDE + to_x, me_width),
            device_id_type=MESH,
        )

    def plane_wait(way):
        some = plane_in.at[pl.ds(0, SIDE * SIDE - 1)]
        pltpu.make_async_copy(some, some, plane_sem.at[way]).wait()

    def start_plane(k):
        send_core(k).wait_recv()
        if k == 0:
            pl.semaphore_wait(know_sem.at[4], SIDE - 1)
        both = total[k, :, core] + core_in[k]
        for to_x in range(SIDE):
            pair[k, to_x] = both[:, to_x * SIDE : (to_x + 1) * SIDE, :]
        if k == 0:
            own_plane.start()
        for d in (2, 1, 3, 0):
            if k or d:
                send_plane(k, (x + d) % SIDE).start()

    def send_ring(e):
        to_deep, to_width = (deep + e // SIDE) % SIDE, (me_width + e % SIDE) % SIDE
        return pltpu.make_async_remote_copy(
            src_ref=plane.at[to_deep],
            dst_ref=deep_in.at[deep * SIDE + me_width],
            send_sem=deep_sem.at[0],
            recv_sem=deep_sem.at[1],
            device_id=(me_layer, to_deep * SIDE + x, to_width),
            device_id_type=MESH,
        )

    def ring_wait(way):
        some = deep_in.at[pl.ds(0, SIDE * SIDE - 1)]
        pltpu.make_async_copy(some, some, deep_sem.at[way]).wait()

    def send_side(d):
        return pltpu.make_async_remote_copy(
            src_ref=side.at[me_width],
            dst_ref=side.at[me_width],
            send_sem=side_sem.at[0, d],
            recv_sem=side_sem.at[1, d],
            device_id=(me_layer, me_feat, (me_width + d) % SIDE),
            device_id_type=MESH,
        )

    encode(0)
    for b in range(blocks):
        split(b)
    load_bias.wait()
    load_db.wait()
    load_tg.wait()
    pass_on(0)
    encode(1)
    encode(2)
    encode(3)
    for l in range(layers):
        side[me_width, l : l + 1, :] = tg[l]
    side[me_width, layers : 2 * layers, :] = db[...]
    for d in range(1, SIDE):
        send_side(d).start()
    know_lines(0)
    pass_on(1)
    finish(0)
    send_core(0).start()
    pass_on(2)
    pass_on(3)
    know_lines(1)
    finish(1)
    send_core(1).start()
    start_plane(0)
    finish(2)
    send_core(2).start()
    start_plane(1)
    know_lines(2)
    finish(3)
    send_core(3).start()
    start_plane(2)
    for d in range(1, SIDE):
        send_side(d).wait_recv()

    @pl.when(is_mid)
    def _():
        pl.semaphore_wait(know_sem.at[3], 1)

    start_plane(3)
    own_plane.wait()
    plane_wait(1)
    summed = jnp.sum(plane_in[...], axis=0)
    for to in range(SIDE):
        for m in range(layers):
            plane[to, m : m + 1, :] = summed[m, to : to + 1, :]
    for e in (8, 9, 10, 11, 4, 12, 5, 6, 7, 13, 14, 15, 1, 2, 3):
        send_ring(e).start()
    deep_in[deep * SIDE + me_width] = plane[deep]
    ring_wait(1)

    sq_error = jnp.zeros((layers, 1), F32)
    sq_target = jnp.zeros((layers, 1), F32)
    for w in range(SIDE):
        whole = deep_in[w]
        for s in range(1, SIDE):
            whole = whole + deep_in[s * SIDE + w]
        wanted = side[w, 0:layers, :]
        diff = whole + side[w, layers : 2 * layers, :] - wanted
        sq_error += jnp.sum(diff * diff, axis=1, keepdims=True)
        sq_target += jnp.sum(wanted * wanted, axis=1, keepdims=True)
    err[...] = sq_error / (sq_target + 1e-06)
    whole = deep_in[me_width]
    for s in range(1, SIDE):
        whole = whole + deep_in[s * SIDE + me_width]
    whole = whole + db[...]
    for m in range(layers):
        recon[m] = whole[m : m + 1]

    gather_wait(0, 0, group - 1)
    plane_wait(0)
    ring_wait(0)
    for d in range(1, SIDE):
        send_side(d).wait_send()
    for k in range(SIDE):
        send_core(k).wait_send()
        for l in range(layers):
            send_part(k, l).wait_send()

            @pl.when(is_mid)
            def _(k=k, l=l):
                send_act(k, l).wait_send()


def per_device(resid, enc_w, enc_b, dec_w, dec_b, target):
    layers, own_rows, wide = resid.shape
    features = enc_w.shape[2]
    blocks, _, width = dec_w.shape
    group = SIDE * CORES
    chunk_rows = CORES * own_rows
    vm = pltpu.VMEM
    dma = pltpu.SemaphoreType.DMA
    in_hbm = pl.BlockSpec(memory_space=pltpu.HBM)
    in_vmem = pl.BlockSpec(memory_space=pltpu.VMEM)
    return pl.pallas_call(
        functools.partial(kernel, layers),
        out_shape=(
            jax.ShapeDtypeStruct((layers, 1, width), F32),
            jax.ShapeDtypeStruct((layers, 1), F32),
        ),
        in_specs=[in_hbm] * 6,
        out_specs=(in_vmem, in_vmem),
        scratch_shapes=[
            vm((layers, own_rows, wide), BF16),
            vm((group, layers, own_rows, wide), BF16),
            vm((layers, wide, features), BF16),
            vm((layers, features), F32),
            vm((blocks, features, width), F32),
            vm((blocks, features, width), BF16),
            vm((blocks, features, width), BF16),
            vm((layers, width), F32),
            vm((layers, 1, width), F32),
            vm((SIDE, layers, chunk_rows, features), F32),
            vm((SIDE, layers, chunk_rows, features), WIRE),
            vm((2, SIDE, layers, chunk_rows, features), WIRE),
            vm((SIDE, layers, chunk_rows, features), WIRE),
            vm((layers, chunk_rows, features), F32),
            vm((SIDE, layers, CORES, own_rows, width), F32),
            vm((SIDE, layers, own_rows, width), F32),
            vm((SIDE, SIDE, layers, SIDE, width), F32),
            vm((SIDE * SIDE, layers, SIDE, width), F32),
            vm((SIDE, layers, width), F32),
            vm((SIDE * SIDE, layers, width), F32),
            vm((SIDE, 2 * layers, width), F32),
            dma((4,)),
            dma((layers,)),
            dma((blocks,)),
            dma((2, SIDE)),
            dma((3, SIDE, layers)),
            dma((2, SIDE, layers)),
            dma((2, SIDE)),
            dma((2,)),
            dma((1,)),
            dma((2,)),
            dma((2, SIDE)),
            pltpu.SemaphoreType.REGULAR((5,)),
        ],
        compiler_params=pltpu.CompilerParams(
            collective_id=0, has_side_effects=True, vmem_limit_bytes=56 * 1024 * 1024
        ),
        cost_estimate=pl.CostEstimate(
            flops=1_400_000_000, bytes_accessed=4_500_000, transcendentals=1_500_000
        ),
    )(resid, enc_w, enc_b, dec_w, dec_b, target)


def solution(mesh):
    in_specs = (
        P(None, "layer", "width"),
        P(None, "width", ("layer", "feat")),
        P(None, ("layer", "feat")),
        P(None, ("layer", "feat"), "width"),
        P(None, "width"),
        P(None, ("layer", "feat"), "width"),
    )
    out_specs = (P(None, ("layer", "feat"), "width"), P(None, ("layer", "feat")))
    return jax.shard_map(
        per_device, mesh=mesh, in_specs=in_specs, out_specs=out_specs, check_vma=False
    )
```

```python
import functools

import jax
import jax.numpy as jnp
from jax import lax
from jax.experimental import pallas as pl
from jax.experimental.pallas import tpu as pltpu
from jax.sharding import PartitionSpec as P

MESH = pl.DeviceIdType.MESH
F32 = jnp.float32
BF16 = jnp.bfloat16
CORES = 2
SIDE = 4
ORDER = ((0, 0), (0, 1), (1, 0), (3, 0), (2, 0), (2, 1), (1, 1), (3, 1))

WIRE = BF16
POWER = 12.0
BASE = 124.0
FINE = 2.0**-10


def to_wire(value):
    size = jnp.exp2(jnp.log2(jnp.abs(value) * (1.0 / FINE) + 1.0) * POWER - BASE)
    return jnp.where(value < 0.0, -size, size).astype(WIRE)


def from_wire(code):
    code = code.astype(F32)
    size = jnp.exp2((jnp.log2(jnp.abs(code)) + BASE) * (1.0 / POWER)) * FINE - FINE
    return jnp.where(code < 0.0, -size, size)


def block_of(target_idx, layer_idx):
    return target_idx * (target_idx + 1) // 2 + layer_idx


def kernel(
    layers,
    resid,
    enc_w,
    enc_b,
    dec_w,
    dec_b,
    target,
    recon,
    own_in,
    rows,
    ew,
    eb,
    dw,
    dw_hi,
    dw_lo,
    db,
    tg,
    part,
    outgoing,
    heard,
    act_wire,
    act,
    total,
    core_in,
    pair,
    plane_in,
    plane,
    deep_in,
    side,
    in_sem,
    ew_sem,
    dw_sem,
    gather_sem,
    part_sem,
    act_sem,
    core_sem,
    plane_sem,
    own_sem,
    deep_sem,
    side_sem,
    know_sem,
):
    me_layer = lax.axis_index("layer")
    me_feat = lax.axis_index("feat")
    me_width = lax.axis_index("width")
    y, core = me_layer // CORES, me_layer % CORES
    deep, x = me_feat // SIDE, me_feat % SIDE
    group = SIDE * CORES
    own_rows = own_in.shape[1]
    features = ew.shape[2]
    blocks = dw.shape[0]
    chunk_rows = CORES * own_rows

    is_low = me_width == 0
    is_high = me_width == SIDE - 1
    is_end = jnp.logical_or(is_low, is_high)
    is_mid = jnp.logical_not(is_end)
    kind = jnp.where(is_mid, 1, 0)
    forward = jnp.where(jnp.logical_or(me_width == 0, me_width == 2), 1, 2)
    outer = jnp.where(me_width == 1, 0, 3)
    beside = jnp.where(is_low, (deep + SIDE - 1) % SIDE, (deep + 1) % SIDE) * SIDE + x

    def signal(sem, layer, feat, wid):
        pl.semaphore_signal(sem, inc=1, device_id=(layer, feat, wid), device_id_type=MESH)

    barrier = pltpu.get_barrier_semaphore()

    load_rows = pltpu.make_async_copy(resid, own_in, in_sem.at[0])
    load_rows.start()
    for d in (4, 3, 5, 2, 6):
        signal(barrier, (me_layer + d) % group, me_feat, me_width)
    for d in range(1, SIDE):
        signal(barrier, me_layer, me_feat, (me_width + d) % SIDE)
    for d in range(1, SIDE):
        signal(barrier, me_layer, deep * SIDE + (x + d) % SIDE, me_width)
    for d in (1, 7):
        signal(barrier, (me_layer + d) % group, me_feat, me_width)

    @pl.when(is_end)
    def _():
        signal(barrier, me_layer, beside, SIDE - 1 - me_width)

    load_bias = pltpu.make_async_copy(enc_b, eb, in_sem.at[1])
    load_db = pltpu.make_async_copy(dec_b, db, in_sem.at[2])
    load_tg = pltpu.make_async_copy(target, tg, in_sem.at[3])
    load_enc = [pltpu.make_async_copy(enc_w.at[l], ew.at[l], ew_sem.at[l]) for l in range(layers)]
    load_dec = [pltpu.make_async_copy(dec_w.at[b], dw.at[b], dw_sem.at[b]) for b in range(blocks)]
    for copy in load_enc + load_dec + [load_bias, load_db, load_tg]:
        copy.start()

    load_rows.wait()
    place = lax.broadcasted_iota(jnp.int32, (own_rows, own_rows), 0)
    source = lax.broadcasted_iota(jnp.int32, (own_rows, own_rows), 1)
    swap = jnp.where(source == (place % SIDE) * SIDE + place // SIDE, 1.0, 0.0).astype(BF16)
    for l in range(layers):
        swapped = jnp.dot(swap, own_in[l], preferred_element_type=F32)
        rows[me_layer, l] = swapped.astype(BF16)

    near = group - 1 + 2 * (SIDE - 1)
    pl.semaphore_wait(barrier, jnp.where(is_end, near + 1, near))

    def push(k, l, to_core):
        pltpu.make_async_remote_copy(
            src_ref=rows.at[me_layer, l],
            dst_ref=rows.at[me_layer, l],
            send_sem=gather_sem.at[0, 0, 0],
            recv_sem=gather_sem.at[1, (SIDE - k) % SIDE, l],
            device_id=(((y + k) % SIDE) * CORES + to_core, me_feat, me_width),
            device_id_type=MESH,
        ).start()

    for k, l in ORDER:
        if k:
            push(k, l, core)
        push(k, l, 1 - core)

    def gather_wait(k, l):
        some = rows.at[pl.ds(0, CORES if k else 1), l]
        pltpu.make_async_copy(some, some, gather_sem.at[1, k, l]).wait()

    def gather_sent():
        some = rows.at[pl.ds(0, group - 1)]
        pltpu.make_async_copy(some, some, gather_sem.at[0, 0, 0]).wait()

    def greet_row(d, carry):
        signal(know_sem.at[4], me_layer, deep * SIDE + (x + d) % SIDE, me_width)
        return carry

    lax.fori_loop(1, SIDE, greet_row, 0)

    @pl.when(is_end)
    def _():
        signal(know_sem.at[0], me_layer, beside, SIDE - 1 - me_width)

    def know_lines(step):
        @pl.when(is_end)
        def _():
            pl.semaphore_wait(know_sem.at[step], 1)
            if step == 0:
                signal(know_sem.at[1], me_layer, me_feat, SIDE - 1 - me_width)
            elif step == 1:
                signal(know_sem.at[2], me_layer, beside, SIDE - 1 - me_width)
            else:
                signal(know_sem.at[3], me_layer, me_feat, forward)

    def split(b):
        load_dec[b].wait()
        step = 64

        def body(i, carry):
            at = pl.ds(pl.multiple_of(i * step, step), step)
            whole = dw[b, at, :]
            high = whole.astype(BF16)
            dw_hi[b, at, :] = high
            dw_lo[b, at, :] = (whole - high.astype(F32)).astype(BF16)
            return carry

        lax.fori_loop(0, features // step, body, 0)

    def send_part(k, l):
        return pltpu.make_async_remote_copy(
            src_ref=outgoing.at[k, l],
            dst_ref=heard.at[kind, k, l],
            send_sem=part_sem.at[0, k, l],
            recv_sem=part_sem.at[1 + kind, k, l],
            device_id=(me_layer, me_feat, forward),
            device_id_type=MESH,
        )

    def wait_part(which, k, l):
        some = heard.at[which, k, l]
        pltpu.make_async_copy(some, some, part_sem.at[1 + which, k, l]).wait()

    def send_act(k, l):
        return pltpu.make_async_remote_copy(
            src_ref=act_wire.at[k, l],
            dst_ref=act_wire.at[k, l],
            send_sem=act_sem.at[0, k, l],
            recv_sem=act_sem.at[1, k, l],
            device_id=(me_layer, me_feat, outer),
            device_id_type=MESH,
        )

    def encode(k, l):
        gather_wait(k, l)
        if k == 0:
            load_enc[l].wait()
        first = ((y + k) % SIDE) * CORES
        some = rows[pl.ds(first, CORES), l].reshape(chunk_rows, -1)
        partial = jnp.dot(some, ew[l], preferred_element_type=F32)

        @pl.when(is_end)
        def _():
            outgoing[k, l] = to_wire(partial)
            send_part(k, l).start()

        @pl.when(is_mid)
        def _():
            part[k, l] = partial

    def pass_on(k, l):
        @pl.when(is_mid)
        def _():
            wait_part(0, k, l)
            summed = part[k, l] + from_wire(heard[0, k, l])
            outgoing[k, l] = to_wire(summed)
            send_part(k, l).start()
            part[k, l] = summed

    def finish(k, l):
        @pl.when(is_mid)
        def _():
            wait_part(1, k, l)
            pre = part[k, l] + from_wire(heard[1, k, l]) + eb[l : l + 1, :]
            pre = jnp.maximum(pre, 0.0)
            act_wire[k, l] = to_wire(pre)
            send_act(k, l).start()
            act[...] = pre

        @pl.when(is_end)
        def _():
            some = act_wire.at[k, l]
            pltpu.make_async_copy(some, some, act_sem.at[1, k, l]).wait()
            act[...] = from_wire(act_wire[k, l])

        decode(k, l)
        send_core(k, l).start()

    def decode(k, l):
        whole = act[...]
        high = whole.astype(BF16)
        low = (whole - high.astype(F32)).astype(BF16)
        both = jnp.concatenate([high, low], axis=0)
        for m in range(l, layers):
            b = block_of(m, l)
            twice = jnp.dot(both, dw_hi[b], preferred_element_type=F32)
            term = twice[:chunk_rows] + twice[chunk_rows:]
            term += jnp.dot(high, dw_lo[b], preferred_element_type=F32)
            term = term.reshape(CORES, own_rows, -1)
            if l == 0:
                total[k, m] = term
            else:
                total[k, m] += term

    def send_core(k, m):
        return pltpu.make_async_remote_copy(
            src_ref=total.at[k, m, 1 - core],
            dst_ref=core_in.at[k, m],
            send_sem=core_sem.at[0, k, m],
            recv_sem=core_sem.at[1, k, m],
            device_id=(y * CORES + 1 - core, me_feat, me_width),
            device_id_type=MESH,
        )

    own_plane = pltpu.make_async_copy(pair.at[0, x], plane_in.at[y * SIDE + x], own_sem.at[0])

    def start_plane(k, m):
        send_core(k, m).wait_recv()
        if (k, m) == ORDER[0]:
            pl.semaphore_wait(know_sem.at[4], SIDE - 1)
        both = total[k, m, core] + core_in[k, m]
        for to_x in range(SIDE):
            pair[k, to_x, m] = both[to_x * SIDE : (to_x + 1) * SIDE, :]
        if (k, m) == (0, layers - 1):
            own_plane.start()
        for d in (2, 1, 3, 0):
            if k or d:
                to_x = (x + d) % SIDE
                pltpu.make_async_remote_copy(
                    src_ref=pair.at[k, to_x, m],
                    dst_ref=plane_in.at[y * SIDE + x, m],
                    send_sem=plane_sem.at[0],
                    recv_sem=plane_sem.at[1],
                    device_id=(((y + k) % SIDE) * CORES + core, deep * SIDE + to_x, me_width),
                    device_id_type=MESH,
                ).start()

    def plane_wait(way):
        some = plane_in.at[pl.ds(0, SIDE * SIDE - 1)]
        pltpu.make_async_copy(some, some, plane_sem.at[way]).wait()

    def send_ring(e):
        to_deep, to_width = (deep + e // SIDE) % SIDE, (me_width + e % SIDE) % SIDE
        return pltpu.make_async_remote_copy(
            src_ref=plane.at[to_deep],
            dst_ref=deep_in.at[deep * SIDE + me_width],
            send_sem=deep_sem.at[0],
            recv_sem=deep_sem.at[1],
            device_id=(me_layer, to_deep * SIDE + x, to_width),
            device_id_type=MESH,
        )

    def ring_wait(way):
        some = deep_in.at[pl.ds(0, SIDE * SIDE - 1)]
        pltpu.make_async_copy(some, some, deep_sem.at[way]).wait()

    def send_side(d):
        return pltpu.make_async_remote_copy(
            src_ref=side.at[me_width],
            dst_ref=side.at[me_width],
            send_sem=side_sem.at[0, d],
            recv_sem=side_sem.at[1, d],
            device_id=(me_layer, me_feat, (me_width + d) % SIDE),
            device_id_type=MESH,
        )

    def share_side():
        load_db.wait()
        load_tg.wait()
        for l in range(layers):
            side[me_width, l : l + 1, :] = tg[l]
        side[me_width, layers : 2 * layers, :] = db[...]
        for d in range(1, SIDE):
            send_side(d).start()

    def ready():
        for b in range(blocks):
            split(b)
        load_bias.wait()

    steps = dict(e=encode, p=pass_on, f=finish, c=start_plane)
    plan = (
        "e0 e1 R e2",
        "e3 p0 e4 p1",
        "e5 e6 e7 S",
        "k0 p2 p3 f0",
        "p4 p5 f1 k1",
        "p6 f2 c0 p7",
        "f3 c1 k2 f4",
        "c2 f5 c3 f6",
        "c4 f7 c5 c6",
    )
    for word in " ".join(plan).split():
        if word == "R":
            ready()
        elif word == "S":
            share_side()
        elif word[0] == "k":
            know_lines(int(word[1]))
        else:
            steps[word[0]](*ORDER[int(word[1])])
    for d in range(1, SIDE):
        send_side(d).wait_recv()
    wanted = [side[w, 0:layers, :] for w in range(SIDE)]
    sq_target = jnp.sum(sum(v * v for v in wanted), axis=1, keepdims=True)
    away = [side[w, layers : 2 * layers, :] - wanted[w] for w in range(SIDE)]

    @pl.when(is_mid)
    def _():
        pl.semaphore_wait(know_sem.at[3], 1)

    start_plane(*ORDER[-1])
    own_plane.wait()
    plane_wait(1)
    summed = jnp.sum(plane_in[...], axis=0)
    for to in range(SIDE):
        for m in range(layers):
            plane[to, m : m + 1, :] = summed[m, to : to + 1, :]
    for e in (8, 9, 10, 11, 4, 12, 5, 6, 7, 13, 14, 15, 1, 2, 3):
        send_ring(e).start()
    deep_in[deep * SIDE + me_width] = plane[deep]
    ring_wait(1)

    squares = jnp.zeros((layers, deep_in.shape[2]), F32)
    for w in range(SIDE):
        whole = deep_in[w]
        for s in range(1, SIDE):
            whole = whole + deep_in[s * SIDE + w]
        diff = whole + away[w]
        squares += diff * diff
    sq_error = jnp.sum(squares, axis=1, keepdims=True)
    ratio = sq_error / (sq_target + 1e-06)
    lane = lax.broadcasted_iota(jnp.int32, (1, whole.shape[1]), 1)
    row = jnp.broadcast_to(ratio[0:1], lane.shape)
    for m in range(1, layers):
        row = jnp.where(lane == m, ratio[m : m + 1], row)
    recon[layers : layers + 1, :] = row
    whole = deep_in[me_width]
    for s in range(1, SIDE):
        whole = whole + deep_in[s * SIDE + me_width]
    whole = whole + db[...]
    recon[0:layers, :] = whole

    gather_sent()
    plane_wait(0)
    ring_wait(0)
    for d in range(1, SIDE):
        send_side(d).wait_send()
    for k, l in ORDER:
        send_core(k, l).wait_send()
        send_part(k, l).wait_send()

        @pl.when(is_mid)
        def _(k=k, l=l):
            send_act(k, l).wait_send()


def divide(layers, both, recon, err):
    for m in range(layers):
        recon[m] = both[m : m + 1, :]
    err[...] = both[layers : layers + 1, 0:layers]


def per_device(resid, enc_w, enc_b, dec_w, dec_b, target):
    layers, own_rows, wide = resid.shape
    features = enc_w.shape[2]
    blocks, _, width = dec_w.shape
    group = SIDE * CORES
    chunk_rows = CORES * own_rows
    vm = pltpu.VMEM
    dma = pltpu.SemaphoreType.DMA
    in_hbm = pl.BlockSpec(memory_space=pltpu.HBM)
    in_vmem = pl.BlockSpec(memory_space=pltpu.VMEM)
    both = pl.pallas_call(
        functools.partial(kernel, layers),
        out_shape=pltpu.VMEM((layers + 1, width), F32),
        in_specs=[in_hbm] * 6,
        out_specs=in_vmem,
        scratch_shapes=[
            vm((layers, own_rows, wide), BF16),
            vm((group, layers, own_rows, wide), BF16),
            vm((layers, wide, features), BF16),
            vm((layers, features), F32),
            vm((blocks, features, width), F32),
            vm((blocks, features, width), BF16),
            vm((blocks, features, width), BF16),
            vm((layers, width), F32),
            vm((layers, 1, width), F32),
            vm((SIDE, layers, chunk_rows, features), F32),
            vm((SIDE, layers, chunk_rows, features), WIRE),
            vm((2, SIDE, layers, chunk_rows, features), WIRE),
            vm((SIDE, layers, chunk_rows, features), WIRE),
            vm((chunk_rows, features), F32),
            vm((SIDE, layers, CORES, own_rows, width), F32),
            vm((SIDE, layers, own_rows, width), F32),
            vm((SIDE, SIDE, layers, SIDE, width), F32),
            vm((SIDE * SIDE, layers, SIDE, width), F32),
            vm((SIDE, layers, width), F32),
            vm((SIDE * SIDE, layers, width), F32),
            vm((SIDE, 2 * layers, width), F32),
            dma((4,)),
            dma((layers,)),
            dma((blocks,)),
            dma((2, SIDE, layers)),
            dma((3, SIDE, layers)),
            dma((2, SIDE, layers)),
            dma((2, SIDE, layers)),
            dma((2,)),
            dma((1,)),
            dma((2,)),
            dma((2, SIDE)),
            pltpu.SemaphoreType.REGULAR((5,)),
        ],
        compiler_params=pltpu.CompilerParams(
            collective_id=0, has_side_effects=True, vmem_limit_bytes=56 * 1024 * 1024
        ),
        cost_estimate=pl.CostEstimate(
            flops=1_400_000_000, bytes_accessed=4_500_000, transcendentals=1_500_000
        ),
    )(resid, enc_w, enc_b, dec_w, dec_b, target)
    recon, err = pl.pallas_call(
        functools.partial(divide, layers),
        out_shape=(
            jax.ShapeDtypeStruct((layers, 1, width), F32),
            jax.ShapeDtypeStruct((1, layers), F32),
        ),
        in_specs=[in_vmem],
        out_specs=(in_vmem, in_vmem),
        compiler_params=pltpu.CompilerParams(vmem_limit_bytes=1024 * 1024),
    )(both)
    return recon, err.reshape(layers, 1)


def solution(mesh):
    in_specs = (
        P(None, "layer", "width"),
        P(None, "width", ("layer", "feat")),
        P(None, ("layer", "feat")),
        P(None, ("layer", "feat"), "width"),
        P(None, "width"),
        P(None, ("layer", "feat"), "width"),
    )
    out_specs = (P(None, ("layer", "feat"), "width"), P(None, ("layer", "feat")))
    return jax.shard_map(
        per_device, mesh=mesh, in_specs=in_specs, out_specs=out_specs, check_vma=False
    )
```

```python
import functools

import jax
import jax.numpy as jnp
from jax import lax
from jax.experimental import pallas as pl
from jax.experimental.pallas import tpu as pltpu
from jax.sharding import PartitionSpec as P

MESH = pl.DeviceIdType.MESH
F32 = jnp.float32
BF16 = jnp.bfloat16
CORES = 2
SIDE = 4
ORDER = ((0, 0), (0, 1), (1, 0), (3, 0), (2, 0), (2, 1), (1, 1), (3, 1))

WIRE = BF16
POWER = 12.0
BASE = 124.0
FINE = 2.0**-10


def to_wire(value):
    size = jnp.exp2(jnp.log2(jnp.abs(value) * (1.0 / FINE) + 1.0) * POWER - BASE)
    return jnp.where(value < 0.0, -size, size).astype(WIRE)


def from_wire(code):
    code = code.astype(F32)
    size = jnp.exp2((jnp.log2(jnp.abs(code)) + BASE) * (1.0 / POWER)) * FINE - FINE
    return jnp.where(code < 0.0, -size, size)


def block_of(target_idx, layer_idx):
    return target_idx * (target_idx + 1) // 2 + layer_idx


def kernel(
    layers,
    resid,
    enc_w,
    enc_b,
    dec_w,
    dec_b,
    target,
    recon,
    own_in,
    rows,
    ew,
    eb,
    dw,
    dw_hi,
    dw_lo,
    db,
    tg,
    part,
    outgoing,
    heard,
    act_wire,
    act,
    total,
    pair,
    plane_in,
    plane,
    deep_in,
    side,
    in_sem,
    ew_sem,
    dw_sem,
    gather_sem,
    part_sem,
    act_sem,
    plane_sem,
    own_sem,
    deep_sem,
    side_sem,
    know_sem,
):
    me_layer = lax.axis_index("layer")
    me_feat = lax.axis_index("feat")
    me_width = lax.axis_index("width")
    y, core = me_layer // CORES, me_layer % CORES
    deep, x = me_feat // SIDE, me_feat % SIDE
    group = SIDE * CORES
    own_rows = own_in.shape[1]
    features = ew.shape[2]
    blocks = dw.shape[0]
    chunk_rows = CORES * own_rows

    is_low = me_width == 0
    is_high = me_width == SIDE - 1
    is_end = jnp.logical_or(is_low, is_high)
    is_mid = jnp.logical_not(is_end)
    kind = jnp.where(is_mid, 1, 0)
    forward = jnp.where(jnp.logical_or(me_width == 0, me_width == 2), 1, 2)
    outer = jnp.where(me_width == 1, 0, 3)
    beside = jnp.where(is_low, (deep + SIDE - 1) % SIDE, (deep + 1) % SIDE) * SIDE + x

    def signal(sem, layer, feat, wid):
        pl.semaphore_signal(sem, inc=1, device_id=(layer, feat, wid), device_id_type=MESH)

    barrier = pltpu.get_barrier_semaphore()

    load_rows = pltpu.make_async_copy(resid, own_in, in_sem.at[0])
    load_rows.start()
    for d in (4, 3, 5, 2, 6):
        signal(barrier, (me_layer + d) % group, me_feat, me_width)
    for d in range(1, SIDE):
        signal(barrier, me_layer, me_feat, (me_width + d) % SIDE)
    for d in range(1, SIDE):
        signal(barrier, me_layer, deep * SIDE + (x + d) % SIDE, me_width)
    for d in (1, 7):
        signal(barrier, (me_layer + d) % group, me_feat, me_width)

    @pl.when(is_end)
    def _():
        signal(barrier, me_layer, beside, SIDE - 1 - me_width)

    load_bias = pltpu.make_async_copy(enc_b, eb, in_sem.at[1])
    load_db = pltpu.make_async_copy(dec_b, db, in_sem.at[2])
    load_tg = pltpu.make_async_copy(target, tg, in_sem.at[3])
    load_enc = [pltpu.make_async_copy(enc_w.at[l], ew.at[l], ew_sem.at[l]) for l in range(layers)]
    load_dec = [pltpu.make_async_copy(dec_w.at[b], dw.at[b], dw_sem.at[b]) for b in range(blocks)]
    for copy in load_enc + load_dec + [load_bias, load_db, load_tg]:
        copy.start()

    load_rows.wait()
    place = lax.broadcasted_iota(jnp.int32, (own_rows, own_rows), 0)
    source = lax.broadcasted_iota(jnp.int32, (own_rows, own_rows), 1)
    swap = jnp.where(source == (place % SIDE) * SIDE + place // SIDE, 1.0, 0.0).astype(BF16)
    for l in range(layers):
        swapped = jnp.dot(swap, own_in[l], preferred_element_type=F32)
        rows[me_layer, l] = swapped.astype(BF16)

    near = group - 1 + 2 * (SIDE - 1)
    pl.semaphore_wait(barrier, jnp.where(is_end, near + 1, near))

    def push(k, l, to_core):
        pltpu.make_async_remote_copy(
            src_ref=rows.at[me_layer, l],
            dst_ref=rows.at[me_layer, l],
            send_sem=gather_sem.at[0, 0, 0],
            recv_sem=gather_sem.at[1, (SIDE - k) % SIDE, l],
            device_id=(((y + k) % SIDE) * CORES + to_core, me_feat, me_width),
            device_id_type=MESH,
        ).start()

    for k, l in ORDER:
        if k:
            push(k, l, core)
        push(k, l, 1 - core)

    def gather_wait(k, l):
        some = rows.at[pl.ds(0, CORES if k else 1), l]
        pltpu.make_async_copy(some, some, gather_sem.at[1, k, l]).wait()

    def gather_sent():
        some = rows.at[pl.ds(0, group - 1)]
        pltpu.make_async_copy(some, some, gather_sem.at[0, 0, 0]).wait()

    def greet_row(d, carry):
        signal(know_sem.at[4], me_layer, deep * SIDE + (x + d) % SIDE, me_width)
        return carry

    lax.fori_loop(1, SIDE, greet_row, 0)

    @pl.when(is_end)
    def _():
        signal(know_sem.at[0], me_layer, beside, SIDE - 1 - me_width)

    def know_lines(step):
        @pl.when(is_end)
        def _():
            pl.semaphore_wait(know_sem.at[step], 1)
            if step == 0:
                signal(know_sem.at[1], me_layer, me_feat, SIDE - 1 - me_width)
            elif step == 1:
                signal(know_sem.at[2], me_layer, beside, SIDE - 1 - me_width)
            else:
                signal(know_sem.at[3], me_layer, me_feat, forward)

    def split(b):
        load_dec[b].wait()
        step = 64

        def body(i, carry):
            at = pl.ds(pl.multiple_of(i * step, step), step)
            whole = dw[b, at, :]
            high = whole.astype(BF16)
            dw_hi[b, at, :] = high
            dw_lo[b, at, :] = (whole - high.astype(F32)).astype(BF16)
            return carry

        lax.fori_loop(0, features // step, body, 0)

    def send_part(k, l):
        return pltpu.make_async_remote_copy(
            src_ref=outgoing.at[k, l],
            dst_ref=heard.at[kind, k, l],
            send_sem=part_sem.at[0, k, l],
            recv_sem=part_sem.at[1 + kind, k, l],
            device_id=(me_layer, me_feat, forward),
            device_id_type=MESH,
        )

    def wait_part(which, k, l):
        some = heard.at[which, k, l]
        pltpu.make_async_copy(some, some, part_sem.at[1 + which, k, l]).wait()

    def send_act(k, l):
        return pltpu.make_async_remote_copy(
            src_ref=act_wire.at[k, l],
            dst_ref=act_wire.at[k, l],
            send_sem=act_sem.at[0, k, l],
            recv_sem=act_sem.at[1, k, l],
            device_id=(me_layer, me_feat, outer),
            device_id_type=MESH,
        )

    def encode(k, l):
        gather_wait(k, l)
        if k == 0:
            load_enc[l].wait()
        first = ((y + k) % SIDE) * CORES
        some = rows[pl.ds(first, CORES), l].reshape(chunk_rows, -1)
        partial = jnp.dot(some, ew[l], preferred_element_type=F32)

        @pl.when(is_end)
        def _():
            outgoing[k, l] = to_wire(partial)
            send_part(k, l).start()

        @pl.when(is_mid)
        def _():
            part[k, l] = partial

    def pass_on(k, l):
        @pl.when(is_mid)
        def _():
            wait_part(0, k, l)
            summed = part[k, l] + from_wire(heard[0, k, l])
            outgoing[k, l] = to_wire(summed)
            send_part(k, l).start()
            part[k, l] = summed

    def finish(k, l):
        @pl.when(is_mid)
        def _():
            wait_part(1, k, l)
            pre = part[k, l] + from_wire(heard[1, k, l]) + eb[l : l + 1, :]
            pre = jnp.maximum(pre, 0.0)
            act_wire[k, l] = to_wire(pre)
            send_act(k, l).start()
            act[...] = pre

        @pl.when(is_end)
        def _():
            some = act_wire.at[k, l]
            pltpu.make_async_copy(some, some, act_sem.at[1, k, l]).wait()
            act[...] = from_wire(act_wire[k, l])

        decode(k, l)

    def decode(k, l):
        whole = act[...]
        high = whole.astype(BF16)
        low = (whole - high.astype(F32)).astype(BF16)
        both = jnp.concatenate([high, low], axis=0)
        for m in range(l, layers):
            b = block_of(m, l)
            twice = jnp.dot(both, dw_hi[b], preferred_element_type=F32)
            term = twice[:chunk_rows] + twice[chunk_rows:]
            term += jnp.dot(high, dw_lo[b], preferred_element_type=F32)
            if l > 0:
                term += total[k, m]
            if m == l:
                start_plane(k, m, term)
            else:
                total[k, m] = term

    mine = me_layer * SIDE + x
    own_plane = [
        pltpu.make_async_copy(pair.at[0, m, core, x], plane_in.at[mine, m], own_sem.at[m])
        for m in range(layers)
    ]

    def start_plane(k, m, summed):
        if (k, m) == ORDER[0]:
            pl.semaphore_wait(know_sem.at[4], SIDE - 1)
        for to_core in range(CORES):
            for to_x in range(SIDE):
                first = to_core * own_rows + to_x * SIDE
                pair[k, m, to_core, to_x] = summed[first : first + SIDE, :]
        if k == 0:
            own_plane[m].start()
        for d in (2, 1, 3, 0):
            for e in range(CORES):
                if k or d or e:
                    to_x, to_core = (x + d) % SIDE, (core + e) % CORES
                    to_layer = ((y + k) % SIDE) * CORES + to_core
                    pltpu.make_async_remote_copy(
                        src_ref=pair.at[k, m, to_core, to_x],
                        dst_ref=plane_in.at[mine, m],
                        send_sem=plane_sem.at[0],
                        recv_sem=plane_sem.at[1],
                        device_id=(to_layer, deep * SIDE + to_x, me_width),
                        device_id_type=MESH,
                    ).start()

    def plane_wait(way):
        some = plane_in.at[pl.ds(0, group * SIDE - 1)]
        pltpu.make_async_copy(some, some, plane_sem.at[way]).wait()

    def send_ring(e):
        to_deep, to_width = (deep + e // SIDE) % SIDE, (me_width + e % SIDE) % SIDE
        return pltpu.make_async_remote_copy(
            src_ref=plane.at[to_deep],
            dst_ref=deep_in.at[deep * SIDE + me_width],
            send_sem=deep_sem.at[0],
            recv_sem=deep_sem.at[1],
            device_id=(me_layer, to_deep * SIDE + x, to_width),
            device_id_type=MESH,
        )

    def ring_wait(way):
        some = deep_in.at[pl.ds(0, SIDE * SIDE - 1)]
        pltpu.make_async_copy(some, some, deep_sem.at[way]).wait()

    def send_side(d):
        return pltpu.make_async_remote_copy(
            src_ref=side.at[me_width],
            dst_ref=side.at[me_width],
            send_sem=side_sem.at[0, d],
            recv_sem=side_sem.at[1, d],
            device_id=(me_layer, me_feat, (me_width + d) % SIDE),
            device_id_type=MESH,
        )

    def share_side():
        load_db.wait()
        load_tg.wait()
        for l in range(layers):
            side[me_width, l : l + 1, :] = tg[l]
        side[me_width, layers : 2 * layers, :] = db[...]
        for d in range(1, SIDE):
            send_side(d).start()

    def ready():
        for b in range(blocks):
            split(b)
        load_bias.wait()

    steps = dict(e=encode, p=pass_on, f=finish)
    plan = (
        "e0 e1 R e2",
        "e3 p0 e4 p1",
        "e5 e6 e7 S",
        "k0 p2 p3 f0",
        "p4 p5 f1 k1",
        "p6 f2 p7 f3",
        "k2 f4 f5 f6",
        "f7",
    )
    for word in " ".join(plan).split():
        if word == "R":
            ready()
        elif word == "S":
            share_side()
        elif word[0] == "k":
            know_lines(int(word[1]))
        else:
            steps[word[0]](*ORDER[int(word[1])])
    for d in range(1, SIDE):
        send_side(d).wait_recv()
    wanted = [side[w, 0:layers, :] for w in range(SIDE)]
    sq_target = jnp.sum(sum(v * v for v in wanted), axis=1, keepdims=True)
    away = [side[w, layers : 2 * layers, :] - wanted[w] for w in range(SIDE)]

    @pl.when(is_mid)
    def _():
        pl.semaphore_wait(know_sem.at[3], 1)

    for m in range(layers):
        own_plane[m].wait()
    plane_wait(1)
    summed = jnp.sum(plane_in[...], axis=0)
    for to in range(SIDE):
        for m in range(layers):
            plane[to, m : m + 1, :] = summed[m, to : to + 1, :]
    for e in (8, 9, 10, 11, 4, 12, 5, 6, 7, 13, 14, 15, 1, 2, 3):
        send_ring(e).start()
    deep_in[deep * SIDE + me_width] = plane[deep]
    ring_wait(1)

    squares = jnp.zeros((layers, deep_in.shape[2]), F32)
    for w in range(SIDE):
        whole = deep_in[w]
        for s in range(1, SIDE):
            whole = whole + deep_in[s * SIDE + w]
        diff = whole + away[w]
        squares += diff * diff
    sq_error = jnp.sum(squares, axis=1, keepdims=True)
    ratio = sq_error / (sq_target + 1e-06)
    lane = lax.broadcasted_iota(jnp.int32, (1, whole.shape[1]), 1)
    row = jnp.broadcast_to(ratio[0:1], lane.shape)
    for m in range(1, layers):
        row = jnp.where(lane == m, ratio[m : m + 1], row)
    recon[layers : layers + 1, :] = row
    whole = deep_in[me_width]
    for s in range(1, SIDE):
        whole = whole + deep_in[s * SIDE + me_width]
    whole = whole + db[...]
    recon[0:layers, :] = whole

    gather_sent()
    plane_wait(0)
    ring_wait(0)
    for d in range(1, SIDE):
        send_side(d).wait_send()
    for k, l in ORDER:
        send_part(k, l).wait_send()

        @pl.when(is_mid)
        def _(k=k, l=l):
            send_act(k, l).wait_send()


def divide(layers, both, recon, err):
    for m in range(layers):
        recon[m] = both[m : m + 1, :]
    err[...] = both[layers : layers + 1, 0:layers]


def per_device(resid, enc_w, enc_b, dec_w, dec_b, target):
    layers, own_rows, wide = resid.shape
    features = enc_w.shape[2]
    blocks, _, width = dec_w.shape
    group = SIDE * CORES
    chunk_rows = CORES * own_rows
    vm = pltpu.VMEM
    dma = pltpu.SemaphoreType.DMA
    in_hbm = pl.BlockSpec(memory_space=pltpu.HBM)
    in_vmem = pl.BlockSpec(memory_space=pltpu.VMEM)
    both = pl.pallas_call(
        functools.partial(kernel, layers),
        out_shape=pltpu.VMEM((layers + 1, width), F32),
        in_specs=[in_hbm] * 6,
        out_specs=in_vmem,
        scratch_shapes=[
            vm((layers, own_rows, wide), BF16),
            vm((group, layers, own_rows, wide), BF16),
            vm((layers, wide, features), BF16),
            vm((layers, features), F32),
            vm((blocks, features, width), F32),
            vm((blocks, features, width), BF16),
            vm((blocks, features, width), BF16),
            vm((layers, width), F32),
            vm((layers, 1, width), F32),
            vm((SIDE, layers, chunk_rows, features), F32),
            vm((SIDE, layers, chunk_rows, features), WIRE),
            vm((2, SIDE, layers, chunk_rows, features), WIRE),
            vm((SIDE, layers, chunk_rows, features), WIRE),
            vm((chunk_rows, features), F32),
            vm((SIDE, layers, chunk_rows, width), F32),
            vm((SIDE, layers, CORES, SIDE, SIDE, width), F32),
            vm((group * SIDE, layers, SIDE, width), F32),
            vm((SIDE, layers, width), F32),
            vm((SIDE * SIDE, layers, width), F32),
            vm((SIDE, 2 * layers, width), F32),
            dma((4,)),
            dma((layers,)),
            dma((blocks,)),
            dma((2, SIDE, layers)),
            dma((3, SIDE, layers)),
            dma((2, SIDE, layers)),
            dma((2,)),
            dma((layers,)),
            dma((2,)),
            dma((2, SIDE)),
            pltpu.SemaphoreType.REGULAR((5,)),
        ],
        compiler_params=pltpu.CompilerParams(
            collective_id=0, has_side_effects=True, vmem_limit_bytes=56 * 1024 * 1024
        ),
        cost_estimate=pl.CostEstimate(
            flops=1_400_000_000, bytes_accessed=4_500_000, transcendentals=1_500_000
        ),
    )(resid, enc_w, enc_b, dec_w, dec_b, target)
    recon, err = pl.pallas_call(
        functools.partial(divide, layers),
        out_shape=(
            jax.ShapeDtypeStruct((layers, 1, width), F32),
            jax.ShapeDtypeStruct((1, layers), F32),
        ),
        in_specs=[in_vmem],
        out_specs=(in_vmem, in_vmem),
        compiler_params=pltpu.CompilerParams(vmem_limit_bytes=1024 * 1024),
    )(both)
    return recon, err.reshape(layers, 1)


def solution(mesh):
    in_specs = (
        P(None, "layer", "width"),
        P(None, "width", ("layer", "feat")),
        P(None, ("layer", "feat")),
        P(None, ("layer", "feat"), "width"),
        P(None, "width"),
        P(None, ("layer", "feat"), "width"),
    )
    out_specs = (P(None, ("layer", "feat"), "width"), P(None, ("layer", "feat")))
    return jax.shard_map(
        per_device, mesh=mesh, in_specs=in_specs, out_specs=out_specs, check_vma=False
    )
```

```python
import functools

import jax
import jax.numpy as jnp
from jax import lax
from jax.experimental import pallas as pl
from jax.experimental.pallas import tpu as pltpu
from jax.sharding import PartitionSpec as P

MESH = pl.DeviceIdType.MESH
F32 = jnp.float32
BF16 = jnp.bfloat16
CORES = 2
SIDE = 4
ORDER = ((0, 0), (0, 1), (2, 0), (2, 1), (1, 0), (3, 0), (1, 1), (3, 1))

WIRE = BF16
POWER = 12.0
BASE = 124.0
FINE = 2.0**-10


def to_wire(value):
    size = jnp.exp2(jnp.log2(jnp.abs(value) * (1.0 / FINE) + 1.0) * POWER - BASE)
    return jnp.where(value < 0.0, -size, size).astype(WIRE)


def from_wire(code):
    code = code.astype(F32)
    size = jnp.exp2((jnp.log2(jnp.abs(code)) + BASE) * (1.0 / POWER)) * FINE - FINE
    return jnp.where(code < 0.0, -size, size)


def block_of(target_idx, layer_idx):
    return target_idx * (target_idx + 1) // 2 + layer_idx


def kernel(
    layers,
    resid,
    enc_w,
    enc_b,
    dec_w,
    dec_b,
    target,
    recon,
    own_in,
    rows,
    ew,
    eb,
    dw,
    dw_hi,
    dw_lo,
    db,
    tg,
    part,
    outgoing,
    heard,
    act_wire,
    act,
    total,
    pair,
    plane_in,
    plane,
    deep_in,
    side,
    in_sem,
    ew_sem,
    dw_sem,
    gather_sem,
    part_sem,
    act_sem,
    plane_sem,
    own_sem,
    deep_sem,
    side_sem,
    know_sem,
):
    me_layer = lax.axis_index("layer")
    me_feat = lax.axis_index("feat")
    me_width = lax.axis_index("width")
    y, core = me_layer // CORES, me_layer % CORES
    deep, x = me_feat // SIDE, me_feat % SIDE
    group = SIDE * CORES
    own_rows = own_in.shape[1]
    features = ew.shape[2]
    blocks = dw.shape[0]
    chunk_rows = CORES * own_rows

    is_low = me_width == 0
    is_high = me_width == SIDE - 1
    is_end = jnp.logical_or(is_low, is_high)
    is_mid = jnp.logical_not(is_end)
    kind = jnp.where(is_mid, 1, 0)
    forward = jnp.where(jnp.logical_or(me_width == 0, me_width == 2), 1, 2)
    outer = jnp.where(me_width == 1, 0, 3)
    beside = jnp.where(is_low, (deep + SIDE - 1) % SIDE, (deep + 1) % SIDE) * SIDE + x

    def signal(sem, layer, feat, wid):
        pl.semaphore_signal(sem, inc=1, device_id=(layer, feat, wid), device_id_type=MESH)

    barrier = pltpu.get_barrier_semaphore()

    load_rows = pltpu.make_async_copy(resid, own_in, in_sem.at[0])
    load_rows.start()
    for d in (4, 3, 5, 2, 6):
        signal(barrier, (me_layer + d) % group, me_feat, me_width)
    for d in range(1, SIDE):
        signal(barrier, me_layer, me_feat, (me_width + d) % SIDE)
    for d in range(1, SIDE):
        signal(barrier, me_layer, deep * SIDE + (x + d) % SIDE, me_width)
    for d in (1, 7):
        signal(barrier, (me_layer + d) % group, me_feat, me_width)

    @pl.when(is_end)
    def _():
        signal(barrier, me_layer, beside, SIDE - 1 - me_width)

    load_bias = pltpu.make_async_copy(enc_b, eb, in_sem.at[1])
    load_db = pltpu.make_async_copy(dec_b, db, in_sem.at[2])
    load_tg = pltpu.make_async_copy(target, tg, in_sem.at[3])
    load_enc = [pltpu.make_async_copy(enc_w.at[l], ew.at[l], ew_sem.at[l]) for l in range(layers)]
    load_dec = [pltpu.make_async_copy(dec_w.at[b], dw.at[b], dw_sem.at[b]) for b in range(blocks)]
    for copy in load_enc + load_dec + [load_bias, load_db, load_tg]:
        copy.start()

    load_rows.wait()
    place = lax.broadcasted_iota(jnp.int32, (own_rows, own_rows), 0)
    source = lax.broadcasted_iota(jnp.int32, (own_rows, own_rows), 1)
    swap = jnp.where(source == (place % SIDE) * SIDE + place // SIDE, 1.0, 0.0).astype(BF16)
    for l in range(layers):
        swapped = jnp.dot(swap, own_in[l], preferred_element_type=F32)
        rows[me_layer, l] = swapped.astype(BF16)

    near = group - 1 + 2 * (SIDE - 1)
    pl.semaphore_wait(barrier, jnp.where(is_end, near + 1, near))

    def push(k, l, to_core):
        pltpu.make_async_remote_copy(
            src_ref=rows.at[me_layer, l],
            dst_ref=rows.at[me_layer, l],
            send_sem=gather_sem.at[0, 0, 0],
            recv_sem=gather_sem.at[1, (SIDE - k) % SIDE, l],
            device_id=(((y + k) % SIDE) * CORES + to_core, me_feat, me_width),
            device_id_type=MESH,
        ).start()

    for k, l in ORDER:
        if k:
            push(k, l, core)
        push(k, l, 1 - core)

    def gather_wait(k, l):
        some = rows.at[pl.ds(0, CORES if k else 1), l]
        pltpu.make_async_copy(some, some, gather_sem.at[1, k, l]).wait()

    def gather_sent():
        some = rows.at[pl.ds(0, group - 1)]
        pltpu.make_async_copy(some, some, gather_sem.at[0, 0, 0]).wait()

    def greet_row(d, carry):
        signal(know_sem.at[4], me_layer, deep * SIDE + (x + d) % SIDE, me_width)
        return carry

    lax.fori_loop(1, SIDE, greet_row, 0)

    @pl.when(is_end)
    def _():
        signal(know_sem.at[0], me_layer, beside, SIDE - 1 - me_width)

    def know_lines(step):
        @pl.when(is_end)
        def _():
            pl.semaphore_wait(know_sem.at[step], 1)
            if step == 0:
                signal(know_sem.at[1], me_layer, me_feat, SIDE - 1 - me_width)
            elif step == 1:
                signal(know_sem.at[2], me_layer, beside, SIDE - 1 - me_width)
            else:
                signal(know_sem.at[3], me_layer, me_feat, forward)

    def split(b):
        load_dec[b].wait()
        step = 64

        def body(i, carry):
            at = pl.ds(pl.multiple_of(i * step, step), step)
            whole = dw[b, at, :]
            high = whole.astype(BF16)
            dw_hi[b, at, :] = high
            dw_lo[b, at, :] = (whole - high.astype(F32)).astype(BF16)
            return carry

        lax.fori_loop(0, features // step, body, 0)

    def send_part(k, l):
        return pltpu.make_async_remote_copy(
            src_ref=outgoing.at[k, l],
            dst_ref=heard.at[kind, k, l],
            send_sem=part_sem.at[0, k, l],
            recv_sem=part_sem.at[1 + kind, k, l],
            device_id=(me_layer, me_feat, forward),
            device_id_type=MESH,
        )

    def wait_part(which, k, l):
        some = heard.at[which, k, l]
        pltpu.make_async_copy(some, some, part_sem.at[1 + which, k, l]).wait()

    def send_act(k, l):
        return pltpu.make_async_remote_copy(
            src_ref=act_wire.at[k, l],
            dst_ref=act_wire.at[k, l],
            send_sem=act_sem.at[0, k, l],
            recv_sem=act_sem.at[1, k, l],
            device_id=(me_layer, me_feat, outer),
            device_id_type=MESH,
        )

    def encode(k, l):
        gather_wait(k, l)
        if k == 0:
            load_enc[l].wait()
        first = ((y + k) % SIDE) * CORES
        some = rows[pl.ds(first, CORES), l].reshape(chunk_rows, -1)
        partial = jnp.dot(some, ew[l], preferred_element_type=F32)

        @pl.when(is_end)
        def _():
            outgoing[k, l] = to_wire(partial)
            send_part(k, l).start()

        @pl.when(is_mid)
        def _():
            part[k, l] = partial

    def pass_on(k, l):
        @pl.when(is_mid)
        def _():
            wait_part(0, k, l)
            summed = part[k, l] + from_wire(heard[0, k, l])
            outgoing[k, l] = to_wire(summed)
            send_part(k, l).start()
            part[k, l] = summed

    def finish(k, l):
        @pl.when(is_mid)
        def _():
            wait_part(1, k, l)
            pre = part[k, l] + from_wire(heard[1, k, l]) + eb[l : l + 1, :]
            pre = jnp.maximum(pre, 0.0)
            act_wire[k, l] = to_wire(pre)
            send_act(k, l).start()
            act[...] = pre

        @pl.when(is_end)
        def _():
            some = act_wire.at[k, l]
            pltpu.make_async_copy(some, some, act_sem.at[1, k, l]).wait()
            act[...] = from_wire(act_wire[k, l])

        decode(k, l)

    def decode(k, l):
        whole = act[...]
        high = whole.astype(BF16)
        low = (whole - high.astype(F32)).astype(BF16)
        both = jnp.concatenate([high, low], axis=0)
        for m in range(l, layers):
            b = block_of(m, l)
            twice = jnp.dot(both, dw_hi[b], preferred_element_type=F32)
            term = twice[:chunk_rows] + twice[chunk_rows:]
            term += jnp.dot(high, dw_lo[b], preferred_element_type=F32)
            if l > 0:
                term += total[k, m]
            if m == l:
                start_plane(k, m, term)
            else:
                total[k, m] = term

    mine = me_layer * SIDE + x
    own_plane = [
        pltpu.make_async_copy(pair.at[0, m, core, x], plane_in.at[mine, m], own_sem.at[m])
        for m in range(layers)
    ]

    def start_plane(k, m, summed):
        if (k, m) == ORDER[0]:
            pl.semaphore_wait(know_sem.at[4], SIDE - 1)
        for to_core in range(CORES):
            for to_x in range(SIDE):
                first = to_core * own_rows + to_x * SIDE
                pair[k, m, to_core, to_x] = summed[first : first + SIDE, :]
        if k == 0:
            own_plane[m].start()
        for d in (2, 1, 3, 0):
            for e in range(CORES):
                if k or d or e:
                    to_x, to_core = (x + d) % SIDE, (core + e) % CORES
                    to_layer = ((y + k) % SIDE) * CORES + to_core
                    pltpu.make_async_remote_copy(
                        src_ref=pair.at[k, m, to_core, to_x],
                        dst_ref=plane_in.at[mine, m],
                        send_sem=plane_sem.at[0],
                        recv_sem=plane_sem.at[1],
                        device_id=(to_layer, deep * SIDE + to_x, me_width),
                        device_id_type=MESH,
                    ).start()

    def plane_wait(way):
        some = plane_in.at[pl.ds(0, group * SIDE - 1)]
        pltpu.make_async_copy(some, some, plane_sem.at[way]).wait()

    def send_ring(e):
        to_deep, to_width = (deep + e // SIDE) % SIDE, (me_width + e % SIDE) % SIDE
        return pltpu.make_async_remote_copy(
            src_ref=plane.at[to_deep],
            dst_ref=deep_in.at[deep * SIDE + me_width],
            send_sem=deep_sem.at[0],
            recv_sem=deep_sem.at[1],
            device_id=(me_layer, to_deep * SIDE + x, to_width),
            device_id_type=MESH,
        )

    def ring_wait(way):
        some = deep_in.at[pl.ds(0, SIDE * SIDE - 1)]
        pltpu.make_async_copy(some, some, deep_sem.at[way]).wait()

    def send_side(d):
        return pltpu.make_async_remote_copy(
            src_ref=side.at[me_width],
            dst_ref=side.at[me_width],
            send_sem=side_sem.at[0, d],
            recv_sem=side_sem.at[1, d],
            device_id=(me_layer, me_feat, (me_width + d) % SIDE),
            device_id_type=MESH,
        )

    def share_side():
        load_db.wait()
        load_tg.wait()
        for l in range(layers):
            side[me_width, l : l + 1, :] = tg[l]
        side[me_width, layers : 2 * layers, :] = db[...]
        for d in range(1, SIDE):
            send_side(d).start()

    def ready():
        for b in range(blocks):
            split(b)
        load_bias.wait()

    steps = dict(e=encode, p=pass_on, f=finish)
    plan = (
        "e0 e1 R e2",
        "e3 p0 e4 p1",
        "e5 e6 e7 S",
        "k0 p2 p3 f0",
        "p4 p5 f1 k1",
        "p6 f2 p7 f3",
        "k2 f4 f5 f6",
        "f7",
    )
    for word in " ".join(plan).split():
        if word == "R":
            ready()
        elif word == "S":
            share_side()
        elif word[0] == "k":
            know_lines(int(word[1]))
        else:
            steps[word[0]](*ORDER[int(word[1])])
    for d in range(1, SIDE):
        send_side(d).wait_recv()
    wanted = [side[w, 0:layers, :] for w in range(SIDE)]
    sq_target = jnp.sum(sum(v * v for v in wanted), axis=1, keepdims=True)
    away = [side[w, layers : 2 * layers, :] - wanted[w] for w in range(SIDE)]

    @pl.when(is_mid)
    def _():
        pl.semaphore_wait(know_sem.at[3], 1)

    for m in range(layers):
        own_plane[m].wait()
    plane_wait(1)
    summed = jnp.sum(plane_in[...], axis=0)
    for to in range(SIDE):
        for m in range(layers):
            plane[to, m : m + 1, :] = summed[m, to : to + 1, :]
    for e in (8, 9, 10, 11, 4, 12, 5, 6, 7, 13, 14, 15, 1, 2, 3):
        send_ring(e).start()
    deep_in[deep * SIDE + me_width] = plane[deep]
    ring_wait(1)

    squares = jnp.zeros((layers, deep_in.shape[2]), F32)
    for w in range(SIDE):
        whole = deep_in[w]
        for s in range(1, SIDE):
            whole = whole + deep_in[s * SIDE + w]
        diff = whole + away[w]
        squares += diff * diff
    sq_error = jnp.sum(squares, axis=1, keepdims=True)
    ratio = sq_error / (sq_target + 1e-06)
    lane = lax.broadcasted_iota(jnp.int32, (1, whole.shape[1]), 1)
    row = jnp.broadcast_to(ratio[0:1], lane.shape)
    for m in range(1, layers):
        row = jnp.where(lane == m, ratio[m : m + 1], row)
    recon[layers : layers + 1, :] = row
    whole = deep_in[me_width]
    for s in range(1, SIDE):
        whole = whole + deep_in[s * SIDE + me_width]
    whole = whole + db[...]
    recon[0:layers, :] = whole

    gather_sent()
    plane_wait(0)
    ring_wait(0)
    for d in range(1, SIDE):
        send_side(d).wait_send()
    for k, l in ORDER:
        send_part(k, l).wait_send()

        @pl.when(is_mid)
        def _(k=k, l=l):
            send_act(k, l).wait_send()


def divide(layers, both, recon, err):
    for m in range(layers):
        recon[m] = both[m : m + 1, :]
    err[...] = both[layers : layers + 1, 0:layers]


def per_device(resid, enc_w, enc_b, dec_w, dec_b, target):
    layers, own_rows, wide = resid.shape
    features = enc_w.shape[2]
    blocks, _, width = dec_w.shape
    group = SIDE * CORES
    chunk_rows = CORES * own_rows
    vm = pltpu.VMEM
    dma = pltpu.SemaphoreType.DMA
    in_hbm = pl.BlockSpec(memory_space=pltpu.HBM)
    in_vmem = pl.BlockSpec(memory_space=pltpu.VMEM)
    both = pl.pallas_call(
        functools.partial(kernel, layers),
        out_shape=pltpu.VMEM((layers + 1, width), F32),
        in_specs=[in_hbm] * 6,
        out_specs=in_vmem,
        scratch_shapes=[
            vm((layers, own_rows, wide), BF16),
            vm((group, layers, own_rows, wide), BF16),
            vm((layers, wide, features), BF16),
            vm((layers, features), F32),
            vm((blocks, features, width), F32),
            vm((blocks, features, width), BF16),
            vm((blocks, features, width), BF16),
            vm((layers, width), F32),
            vm((layers, 1, width), F32),
            vm((SIDE, layers, chunk_rows, features), F32),
            vm((SIDE, layers, chunk_rows, features), WIRE),
            vm((2, SIDE, layers, chunk_rows, features), WIRE),
            vm((SIDE, layers, chunk_rows, features), WIRE),
            vm((chunk_rows, features), F32),
            vm((SIDE, layers, chunk_rows, width), F32),
            vm((SIDE, layers, CORES, SIDE, SIDE, width), F32),
            vm((group * SIDE, layers, SIDE, width), F32),
            vm((SIDE, layers, width), F32),
            vm((SIDE * SIDE, layers, width), F32),
            vm((SIDE, 2 * layers, width), F32),
            dma((4,)),
            dma((layers,)),
            dma((blocks,)),
            dma((2, SIDE, layers)),
            dma((3, SIDE, layers)),
            dma((2, SIDE, layers)),
            dma((2,)),
            dma((layers,)),
            dma((2,)),
            dma((2, SIDE)),
            pltpu.SemaphoreType.REGULAR((5,)),
        ],
        compiler_params=pltpu.CompilerParams(
            collective_id=0, has_side_effects=True, vmem_limit_bytes=56 * 1024 * 1024
        ),
        cost_estimate=pl.CostEstimate(
            flops=1_400_000_000, bytes_accessed=4_500_000, transcendentals=1_500_000
        ),
    )(resid, enc_w, enc_b, dec_w, dec_b, target)
    recon, err = pl.pallas_call(
        functools.partial(divide, layers),
        out_shape=(
            jax.ShapeDtypeStruct((layers, 1, width), F32),
            jax.ShapeDtypeStruct((1, layers), F32),
        ),
        in_specs=[in_vmem],
        out_specs=(in_vmem, in_vmem),
        compiler_params=pltpu.CompilerParams(vmem_limit_bytes=1024 * 1024),
    )(both)
    return recon, err.reshape(layers, 1)


def solution(mesh):
    in_specs = (
        P(None, "layer", "width"),
        P(None, "width", ("layer", "feat")),
        P(None, ("layer", "feat")),
        P(None, ("layer", "feat"), "width"),
        P(None, "width"),
        P(None, ("layer", "feat"), "width"),
    )
    out_specs = (P(None, ("layer", "feat"), "width"), P(None, ("layer", "feat")))
    return jax.shard_map(
        per_device, mesh=mesh, in_specs=in_specs, out_specs=out_specs, check_vma=False
    )
```

```python
import functools

import jax
import jax.numpy as jnp
from jax import lax
from jax.experimental import pallas as pl
from jax.experimental.pallas import tpu as pltpu
from jax.sharding import PartitionSpec as P

MESH = pl.DeviceIdType.MESH
F32 = jnp.float32
BF16 = jnp.bfloat16
CORES = 2
SIDE = 4
ORDER = ((0, 0), (0, 1), (2, 0), (2, 1), (1, 0), (3, 0), (1, 1), (3, 1))

WIRE = BF16
POWER = 12.0
BASE = 124.0
FINE = 2.0**-10


PIECES = 2


def to_wire(value):
    size = jnp.exp2(jnp.log2(jnp.abs(value) * (1.0 / FINE) + 1.0) * POWER - BASE)
    return jnp.where(value < 0.0, -size, size).astype(WIRE)


def from_wire(code):
    code = code.astype(F32)
    size = jnp.exp2((jnp.log2(jnp.abs(code)) + BASE) * (1.0 / POWER)) * FINE - FINE
    return jnp.where(code < 0.0, -size, size)


def block_of(target_idx, layer_idx):
    return target_idx * (target_idx + 1) // 2 + layer_idx


def kernel(
    layers,
    resid,
    enc_w,
    enc_b,
    dec_w,
    dec_b,
    target,
    recon,
    own_in,
    rows,
    ew,
    eb,
    dw,
    dw_hi,
    dw_lo,
    db,
    tg,
    part,
    outgoing,
    heard,
    act_wire,
    act,
    total,
    pair,
    plane_in,
    plane,
    deep_in,
    side,
    in_sem,
    ew_sem,
    dw_sem,
    gather_sem,
    part_sem,
    act_sem,
    plane_sem,
    own_sem,
    deep_sem,
    side_sem,
    know_sem,
):
    me_layer = lax.axis_index("layer")
    me_feat = lax.axis_index("feat")
    me_width = lax.axis_index("width")
    y, core = me_layer // CORES, me_layer % CORES
    deep, x = me_feat // SIDE, me_feat % SIDE
    group = SIDE * CORES
    own_rows = own_in.shape[1]
    features = ew.shape[2]
    blocks = dw.shape[0]
    chunk_rows = CORES * own_rows
    wide = features // PIECES

    is_low = me_width == 0
    is_high = me_width == SIDE - 1
    is_end = jnp.logical_or(is_low, is_high)
    is_mid = jnp.logical_not(is_end)
    kind = jnp.where(is_mid, 1, 0)
    forward = jnp.where(jnp.logical_or(me_width == 0, me_width == 2), 1, 2)
    outer = jnp.where(me_width == 1, 0, 3)
    beside = jnp.where(is_low, (deep + SIDE - 1) % SIDE, (deep + 1) % SIDE) * SIDE + x

    def signal(sem, layer, feat, wid):
        pl.semaphore_signal(sem, inc=1, device_id=(layer, feat, wid), device_id_type=MESH)

    barrier = pltpu.get_barrier_semaphore()

    load_rows = pltpu.make_async_copy(resid, own_in, in_sem.at[0])
    load_rows.start()
    for d in (4, 3, 5, 2, 6):
        signal(barrier, (me_layer + d) % group, me_feat, me_width)
    for d in range(1, SIDE):
        signal(barrier, me_layer, me_feat, (me_width + d) % SIDE)
    for d in range(1, SIDE):
        signal(barrier, me_layer, deep * SIDE + (x + d) % SIDE, me_width)
    for d in (1, 7):
        signal(barrier, (me_layer + d) % group, me_feat, me_width)

    @pl.when(is_end)
    def _():
        signal(barrier, me_layer, beside, SIDE - 1 - me_width)

    load_bias = pltpu.make_async_copy(enc_b, eb, in_sem.at[1])
    load_db = pltpu.make_async_copy(dec_b, db, in_sem.at[2])
    load_tg = pltpu.make_async_copy(target, tg, in_sem.at[3])
    load_enc = [pltpu.make_async_copy(enc_w.at[l], ew.at[l], ew_sem.at[l]) for l in range(layers)]
    load_dec = [pltpu.make_async_copy(dec_w.at[b], dw.at[b], dw_sem.at[b]) for b in range(blocks)]
    for copy in load_enc + load_dec + [load_bias, load_db, load_tg]:
        copy.start()

    load_rows.wait()
    place = lax.broadcasted_iota(jnp.int32, (own_rows, own_rows), 0)
    source = lax.broadcasted_iota(jnp.int32, (own_rows, own_rows), 1)
    swap = jnp.where(source == (place % SIDE) * SIDE + place // SIDE, 1.0, 0.0).astype(BF16)
    for l in range(layers):
        swapped = jnp.dot(swap, own_in[l], preferred_element_type=F32)
        rows[me_layer, l] = swapped.astype(BF16)

    near = group - 1 + 2 * (SIDE - 1)
    pl.semaphore_wait(barrier, jnp.where(is_end, near + 1, near))

    def push(k, l, to_core):
        pltpu.make_async_remote_copy(
            src_ref=rows.at[me_layer, l],
            dst_ref=rows.at[me_layer, l],
            send_sem=gather_sem.at[0, 0, 0],
            recv_sem=gather_sem.at[1, (SIDE - k) % SIDE, l],
            device_id=(((y + k) % SIDE) * CORES + to_core, me_feat, me_width),
            device_id_type=MESH,
        ).start()

    for k, l in ORDER:
        if k:
            push(k, l, core)
        push(k, l, 1 - core)

    def gather_wait(k, l):
        some = rows.at[pl.ds(0, CORES if k else 1), l]
        pltpu.make_async_copy(some, some, gather_sem.at[1, k, l]).wait()

    def gather_sent():
        some = rows.at[pl.ds(0, group - 1)]
        pltpu.make_async_copy(some, some, gather_sem.at[0, 0, 0]).wait()

    def greet_row(d, carry):
        signal(know_sem.at[4], me_layer, deep * SIDE + (x + d) % SIDE, me_width)
        return carry

    lax.fori_loop(1, SIDE, greet_row, 0)

    @pl.when(is_end)
    def _():
        signal(know_sem.at[0], me_layer, beside, SIDE - 1 - me_width)

    def know_lines(step):
        @pl.when(is_end)
        def _():
            pl.semaphore_wait(know_sem.at[step], 1)
            if step == 0:
                signal(know_sem.at[1], me_layer, me_feat, SIDE - 1 - me_width)
            elif step == 1:
                signal(know_sem.at[2], me_layer, beside, SIDE - 1 - me_width)
            else:
                signal(know_sem.at[3], me_layer, me_feat, forward)

    def split(b):
        load_dec[b].wait()
        step = 64

        def body(i, carry):
            at = pl.ds(pl.multiple_of(i * step, step), step)
            whole = dw[b, at, :]
            high = whole.astype(BF16)
            dw_hi[b, at, :] = high
            dw_lo[b, at, :] = (whole - high.astype(F32)).astype(BF16)
            return carry

        lax.fori_loop(0, features // step, body, 0)

    def send_part(k, l, h):
        return pltpu.make_async_remote_copy(
            src_ref=outgoing.at[k, l, h],
            dst_ref=heard.at[kind, k, l, h],
            send_sem=part_sem.at[0, k, l, h],
            recv_sem=part_sem.at[1 + kind, k, l, h],
            device_id=(me_layer, me_feat, forward),
            device_id_type=MESH,
        )

    def wait_part(which, k, l, h):
        some = heard.at[which, k, l, h]
        pltpu.make_async_copy(some, some, part_sem.at[1 + which, k, l, h]).wait()

    def send_act(k, l, h):
        return pltpu.make_async_remote_copy(
            src_ref=act_wire.at[k, l, h],
            dst_ref=act_wire.at[k, l, h],
            send_sem=act_sem.at[0, k, l, h],
            recv_sem=act_sem.at[1, k, l, h],
            device_id=(me_layer, me_feat, outer),
            device_id_type=MESH,
        )

    def encode(k, l):
        gather_wait(k, l)
        if k == 0:
            load_enc[l].wait()
        first = ((y + k) % SIDE) * CORES
        some = rows[pl.ds(first, CORES), l].reshape(chunk_rows, -1)
        for h in range(PIECES):
            weights = ew[l, :, h * wide : (h + 1) * wide]
            partial = jnp.dot(some, weights, preferred_element_type=F32)

            @pl.when(is_end)
            def _(h=h, partial=partial):
                outgoing[k, l, h] = to_wire(partial)
                send_part(k, l, h).start()

            @pl.when(is_mid)
            def _(h=h, partial=partial):
                part[k, l, h] = partial

    def pass_on(k, l):
        @pl.when(is_mid)
        def _():
            for h in range(PIECES):
                wait_part(0, k, l, h)
                summed = part[k, l, h] + from_wire(heard[0, k, l, h])
                outgoing[k, l, h] = to_wire(summed)
                send_part(k, l, h).start()
                part[k, l, h] = summed

    def finish(k, l):
        terms = {}
        for h in range(PIECES):

            @pl.when(is_mid)
            def _(h=h):
                wait_part(1, k, l, h)
                bias = eb[l : l + 1, h * wide : (h + 1) * wide]
                pre = part[k, l, h] + from_wire(heard[1, k, l, h]) + bias
                pre = jnp.maximum(pre, 0.0)
                act_wire[k, l, h] = to_wire(pre)
                send_act(k, l, h).start()
                act[h] = pre

            @pl.when(is_end)
            def _(h=h):
                some = act_wire.at[k, l, h]
                pltpu.make_async_copy(some, some, act_sem.at[1, k, l, h]).wait()
                act[h] = from_wire(act_wire[k, l, h])

            decode(l, h, terms)
        for m in range(l, layers):
            term = terms[m]
            if l > 0:
                term += total[k, m]
            if m == l:
                start_plane(k, m, term)
            else:
                total[k, m] = term

    def decode(l, h, terms):
        whole = act[h]
        high = whole.astype(BF16)
        low = (whole - high.astype(F32)).astype(BF16)
        both = jnp.concatenate([high, low], axis=0)
        at = slice(h * wide, (h + 1) * wide)
        for m in range(l, layers):
            b = block_of(m, l)
            twice = jnp.dot(both, dw_hi[b, at, :], preferred_element_type=F32)
            term = twice[:chunk_rows] + twice[chunk_rows:]
            term += jnp.dot(high, dw_lo[b, at, :], preferred_element_type=F32)
            terms[m] = terms[m] + term if m in terms else term

    mine = me_layer * SIDE + x
    own_plane = [
        pltpu.make_async_copy(pair.at[0, m, core, x], plane_in.at[mine, m], own_sem.at[m])
        for m in range(layers)
    ]

    def start_plane(k, m, summed):
        if (k, m) == ORDER[0]:
            pl.semaphore_wait(know_sem.at[4], SIDE - 1)
        for to_core in range(CORES):
            for to_x in range(SIDE):
                first = to_core * own_rows + to_x * SIDE
                pair[k, m, to_core, to_x] = summed[first : first + SIDE, :]
        if k == 0:
            own_plane[m].start()
        for d in (2, 1, 3, 0):
            for e in range(CORES):
                if k or d or e:
                    to_x, to_core = (x + d) % SIDE, (core + e) % CORES
                    to_layer = ((y + k) % SIDE) * CORES + to_core
                    pltpu.make_async_remote_copy(
                        src_ref=pair.at[k, m, to_core, to_x],
                        dst_ref=plane_in.at[mine, m],
                        send_sem=plane_sem.at[0, m],
                        recv_sem=plane_sem.at[1, m],
                        device_id=(to_layer, deep * SIDE + to_x, me_width),
                        device_id_type=MESH,
                    ).start()

    def plane_wait(way, m):
        some = plane_in.at[pl.ds(0, group * SIDE - 1), m]
        pltpu.make_async_copy(some, some, plane_sem.at[way, m]).wait()

    def send_ring(e):
        to_deep, to_width = (deep + e // SIDE) % SIDE, (me_width + e % SIDE) % SIDE
        return pltpu.make_async_remote_copy(
            src_ref=plane.at[to_deep],
            dst_ref=deep_in.at[deep * SIDE + me_width],
            send_sem=deep_sem.at[0],
            recv_sem=deep_sem.at[1],
            device_id=(me_layer, to_deep * SIDE + x, to_width),
            device_id_type=MESH,
        )

    def ring_wait(way):
        some = deep_in.at[pl.ds(0, SIDE * SIDE - 1)]
        pltpu.make_async_copy(some, some, deep_sem.at[way]).wait()

    def send_side(d):
        return pltpu.make_async_remote_copy(
            src_ref=side.at[me_width],
            dst_ref=side.at[me_width],
            send_sem=side_sem.at[0, d],
            recv_sem=side_sem.at[1, d],
            device_id=(me_layer, me_feat, (me_width + d) % SIDE),
            device_id_type=MESH,
        )

    def share_side():
        load_db.wait()
        load_tg.wait()
        for l in range(layers):
            side[me_width, l : l + 1, :] = tg[l]
        side[me_width, layers : 2 * layers, :] = db[...]
        for d in range(1, SIDE):
            send_side(d).start()

    def ready():
        for b in range(blocks):
            split(b)
        load_bias.wait()

    steps = dict(e=encode, p=pass_on, f=finish)
    plan = (
        "e0 e1 R e2",
        "e3 p0 e4 p1",
        "e5 e6 e7 S",
        "k0 p2 p3 f0",
        "p4 p5 f1 k1",
        "p6 f2 p7 f3",
        "k2 f4 f5 f6",
        "f7",
    )
    for word in " ".join(plan).split():
        if word == "R":
            ready()
        elif word == "S":
            share_side()
        elif word[0] == "k":
            know_lines(int(word[1]))
        else:
            steps[word[0]](*ORDER[int(word[1])])
    for d in range(1, SIDE):
        send_side(d).wait_recv()
    wanted = [side[w, 0:layers, :] for w in range(SIDE)]
    sq_target = jnp.sum(sum(v * v for v in wanted), axis=1, keepdims=True)
    away = [side[w, layers : 2 * layers, :] - wanted[w] for w in range(SIDE)]

    @pl.when(is_mid)
    def _():
        pl.semaphore_wait(know_sem.at[3], 1)

    for m in range(layers):
        own_plane[m].wait()
        plane_wait(1, m)
        summed = jnp.sum(plane_in[:, m], axis=0)
        for to in range(SIDE):
            plane[to, m : m + 1, :] = summed[to : to + 1, :]
    for e in (8, 9, 10, 11, 4, 12, 5, 6, 7, 13, 14, 15, 1, 2, 3):
        send_ring(e).start()
    deep_in[deep * SIDE + me_width] = plane[deep]
    ring_wait(1)

    squares = jnp.zeros((layers, deep_in.shape[2]), F32)
    for w in range(SIDE):
        whole = deep_in[w]
        for s in range(1, SIDE):
            whole = whole + deep_in[s * SIDE + w]
        diff = whole + away[w]
        squares += diff * diff
    sq_error = jnp.sum(squares, axis=1, keepdims=True)
    ratio = sq_error / (sq_target + 1e-06)
    lane = lax.broadcasted_iota(jnp.int32, (1, whole.shape[1]), 1)
    row = jnp.broadcast_to(ratio[0:1], lane.shape)
    for m in range(1, layers):
        row = jnp.where(lane == m, ratio[m : m + 1], row)
    recon[layers : layers + 1, :] = row
    whole = deep_in[me_width]
    for s in range(1, SIDE):
        whole = whole + deep_in[s * SIDE + me_width]
    whole = whole + db[...]
    recon[0:layers, :] = whole

    gather_sent()
    for m in range(layers):
        plane_wait(0, m)
    ring_wait(0)
    for d in range(1, SIDE):
        send_side(d).wait_send()
    for k, l in ORDER:
        for h in range(PIECES):
            send_part(k, l, h).wait_send()

            @pl.when(is_mid)
            def _(k=k, l=l, h=h):
                send_act(k, l, h).wait_send()


def divide(layers, both, recon, err):
    for m in range(layers):
        recon[m] = both[m : m + 1, :]
    err[...] = both[layers : layers + 1, 0:layers]


def per_device(resid, enc_w, enc_b, dec_w, dec_b, target):
    layers, own_rows, wide = resid.shape
    features = enc_w.shape[2]
    blocks, _, width = dec_w.shape
    group = SIDE * CORES
    chunk_rows = CORES * own_rows
    piece = (PIECES, chunk_rows, features // PIECES)
    vm = pltpu.VMEM
    dma = pltpu.SemaphoreType.DMA
    in_hbm = pl.BlockSpec(memory_space=pltpu.HBM)
    in_vmem = pl.BlockSpec(memory_space=pltpu.VMEM)
    both = pl.pallas_call(
        functools.partial(kernel, layers),
        out_shape=pltpu.VMEM((layers + 1, width), F32),
        in_specs=[in_hbm] * 6,
        out_specs=in_vmem,
        scratch_shapes=[
            vm((layers, own_rows, wide), BF16),
            vm((group, layers, own_rows, wide), BF16),
            vm((layers, wide, features), BF16),
            vm((layers, features), F32),
            vm((blocks, features, width), F32),
            vm((blocks, features, width), BF16),
            vm((blocks, features, width), BF16),
            vm((layers, width), F32),
            vm((layers, 1, width), F32),
            vm((SIDE, layers) + piece, F32),
            vm((SIDE, layers) + piece, WIRE),
            vm((2, SIDE, layers) + piece, WIRE),
            vm((SIDE, layers) + piece, WIRE),
            vm(piece, F32),
            vm((SIDE, layers, chunk_rows, width), F32),
            vm((SIDE, layers, CORES, SIDE, SIDE, width), F32),
            vm((group * SIDE, layers, SIDE, width), F32),
            vm((SIDE, layers, width), F32),
            vm((SIDE * SIDE, layers, width), F32),
            vm((SIDE, 2 * layers, width), F32),
            dma((4,)),
            dma((layers,)),
            dma((blocks,)),
            dma((2, SIDE, layers)),
            dma((3, SIDE, layers, PIECES)),
            dma((2, SIDE, layers, PIECES)),
            dma((2, layers)),
            dma((layers,)),
            dma((2,)),
            dma((2, SIDE)),
            pltpu.SemaphoreType.REGULAR((5,)),
        ],
        compiler_params=pltpu.CompilerParams(
            collective_id=0, has_side_effects=True, vmem_limit_bytes=56 * 1024 * 1024
        ),
        cost_estimate=pl.CostEstimate(
            flops=1_400_000_000, bytes_accessed=4_500_000, transcendentals=1_500_000
        ),
    )(resid, enc_w, enc_b, dec_w, dec_b, target)
    recon, err = pl.pallas_call(
        functools.partial(divide, layers),
        out_shape=(
            jax.ShapeDtypeStruct((layers, 1, width), F32),
            jax.ShapeDtypeStruct((1, layers), F32),
        ),
        in_specs=[in_vmem],
        out_specs=(in_vmem, in_vmem),
        compiler_params=pltpu.CompilerParams(vmem_limit_bytes=1024 * 1024),
    )(both)
    return recon, err.reshape(layers, 1)


def solution(mesh):
    in_specs = (
        P(None, "layer", "width"),
        P(None, "width", ("layer", "feat")),
        P(None, ("layer", "feat")),
        P(None, ("layer", "feat"), "width"),
        P(None, "width"),
        P(None, ("layer", "feat"), "width"),
    )
    out_specs = (P(None, ("layer", "feat"), "width"), P(None, ("layer", "feat")))
    return jax.shard_map(
        per_device, mesh=mesh, in_specs=in_specs, out_specs=out_specs, check_vma=False
    )
```
